256 devices in a mesh: pb: 4 (over y_lo, core), ta: 64 (over y_hi, z, x).
Axes of the slice: x: 4, y: 4 (y_hi: 2, y_lo: 2; y = y_hi * 2 + y_lo), z: 8, core: 2. Of those that a mesh axis runs over, the one named last changes fastest.
Arguments:
- source_feats: bfloat16 [128, 512, 128], P('pb', 'ta'), may hold values from -36 to 36, as said below
- target_feats: bfloat16 [128, 65536], P(None, 'ta'), may hold values from -36 to 36, as said below
- back_flow: bfloat16 [2, 65536], P(None, 'ta'), may hold values from -1.1953125 to 1.1953125
- attn_weights: bfloat16 [2, 4, 128, 128], replicated, may hold values from -0.5 to 0.5
- norm_gain: float32 [2, 128], replicated, may hold values from 0.1 to 1.9
- fetch_list: int32 [256, 4], P(('pb', 'ta')), may hold values from 0 to 63
- dest_local: int32 [128, 512], P('pb', 'ta'), may hold values from 0 to 4095
Outputs:
- flow_field: float32 [2, 128, 512], P(None, 'pb', 'ta')
- consistency: float32 [128, 512], P('pb', 'ta')
The draws below stay inside these ranges and needn't reach their ends.
Inputs may be any that keep to these rules, and one draw needn't show every extreme that they name: `source_feats`: feature values. `target_feats`: feature values.
All inputs are finite; a program needn't handle non-finite values.
Results may differ from the reference program's by a relative error of at most 0.029.
The reference program's roundings to bfloat16 on the way count: a program that leaves them out, or rounds other values in their place, can miss the bound.
Values may be sent and summed in bfloat16 or wider, within the bound.
A program may use at most 128 MiB of HBM per device.

```python
import math
import jax
import jax.numpy as jnp
from jax import lax

C = 128
WIN = 8
TQH = 32
TQW = 8
K = 4
HQ = 128
WQ = 512
TB = 1024
NT = 65536
N_PB = 4
N_TA = 64


def draw_source_feats(key, part):
    key = jax.random.fold_in(key, 5)
    values = jnp.clip(jax.random.normal(key, (HQ, WQ, C), jnp.float32), -4.0, 4.0)
    return values.astype(jnp.bfloat16)


def draw_target_feats(key, part):
    key = jax.random.fold_in(key, 6)
    values = jnp.clip(jax.random.normal(key, (C, NT), jnp.float32), -4.0, 4.0)
    return values.astype(jnp.bfloat16)


def with_ends(array, own_key, least, high):
    place = [jax.random.randint(jax.random.fold_in(own_key, axis), (), 0, length) for axis, length in enumerate(array.shape)]
    longest = array.shape.index(max(array.shape))
    next_to = place[:longest] + [(place[longest] + 1) % array.shape[longest]] + place[longest + 1:]
    return array.at[tuple(place)].set(least).at[tuple(next_to)].set(high)


def level_of(rng, shape, pieces, low, largest):
    gain, own = 1.0, jax.random.fold_in(rng, 6)
    for dim, shards_of in pieces:
        steps = jnp.exp(jax.random.uniform(jax.random.fold_in(own, dim), (shards_of,), jnp.float32, low / len(pieces), largest / len(pieces)))
        gain = gain * jnp.repeat(steps, shape[dim] // shards_of).reshape([-1 if axis == dim else 1 for axis in range(len(shape))])
    return gain


def gaussian(stream_key, extent, scale, limit, split=(), kind=jnp.bfloat16):
    entries = jax.random.normal(stream_key, extent, jnp.float32) * scale
    if len(split) > 0:
        entries = level_of(stream_key, extent, split, -0.22, 0.18) * entries
    return jnp.clip(entries, min=-limit, max=limit).astype(kind)


def setup_inputs(seed: int = 0) -> dict:
    keys = jax.random.split(jax.random.key(seed), 8)
    return {
        "source_feats": draw_source_feats(jax.random.fold_in(keys[7], 71), 0),
        "target_feats": draw_target_feats(jax.random.fold_in(keys[7], 71), 0),
        "back_flow": gaussian(keys[2], (2, NT), 0.3, 1.1953125, ((1, 64),)),
        "attn_weights": gaussian(keys[3], (2, 4, C, C), C ** -0.5, 0.5),
        "norm_gain": jnp.clip(1.0 + 0.18 * jax.random.normal(keys[4], (2, C), jnp.float32), 0.1, 1.9),
        "fetch_list": with_ends(jax.random.randint(keys[5], (N_PB * N_TA, K), 0, N_TA), jax.random.fold_in(keys[5], 1), 0, N_TA - 1).astype(jnp.int32),
        "dest_local": with_ends(jax.random.randint(keys[6], (HQ, WQ), 0, K * TB), jax.random.fold_in(keys[6], 1), 0, (K * TB) - 1).astype(jnp.int32),
    }


NORM_EPSILON = 1e-05
MATCH_GAIN = 2.0
FLOW_ALPHA = 0.01
FLOW_BETA = 0.5

def layer_norm(values, gains):
    center = values - lax.optimization_barrier(jnp.mean(values, axis=-1, keepdims=True))
    spread = lax.optimization_barrier(jnp.mean(center * center, axis=-1, keepdims=True))
    return center * lax.rsqrt(spread + NORM_EPSILON) * gains

def to_windows(picture):
    img_rows, img_cols = (picture.shape[0], picture.shape[1])
    trailing = picture.shape[2:]
    blocked = picture.reshape((img_rows // WIN, WIN, img_cols // WIN, WIN) + trailing)
    blocked = jnp.swapaxes(blocked, 1, 2)
    return blocked.reshape((img_rows // WIN * (img_cols // WIN), WIN * WIN) + trailing)

def from_windows(windows, img_rows, img_cols):
    trailing = windows.shape[2:]
    blocked = windows.reshape((img_rows // WIN, img_cols // WIN, WIN, WIN) + trailing)
    return jnp.swapaxes(blocked, 1, 2).reshape((img_rows, img_cols) + trailing)

def window_section(picture, labels, matrices, norm_gains):
    img_rows, img_cols, channels = picture.shape
    windows = to_windows(picture)
    win_count, tokens = (windows.shape[0], windows.shape[1])
    pixels = windows.reshape(-1, channels)
    projected = [jnp.dot(pixels, matrices[matrix_id], preferred_element_type=jnp.float32).astype(jnp.bfloat16).reshape(win_count, tokens, channels) for matrix_id in range(3)]
    scores = jnp.einsum('wic,wjc->wij', projected[0].astype(jnp.float32), projected[1].astype(jnp.float32)) / math.sqrt(channels)
    if labels is not None:
        region_tags = to_windows(labels)
        admitted = region_tags[:, :, None] == region_tags[:, None, :]
        scores = jnp.where(admitted, scores, -jnp.inf)
    highest = lax.optimization_barrier(jnp.max(scores, axis=-1, keepdims=True))
    raised = jnp.exp(scores - highest)
    attention = (raised / lax.optimization_barrier(jnp.sum(raised, axis=-1, keepdims=True))).astype(jnp.bfloat16)
    attended = jnp.einsum('wij,wjc->wic', attention.astype(jnp.float32), projected[2].astype(jnp.float32)).astype(jnp.bfloat16)
    message = jnp.dot(attended.reshape(-1, channels), matrices[3], preferred_element_type=jnp.float32)
    updated = pixels.astype(jnp.float32) + layer_norm(message, norm_gains)
    return from_windows(updated.astype(jnp.bfloat16).reshape(win_count, tokens, channels), img_rows, img_cols)

def coord_table(columns, frame_rows, frame_cols):
    rows_norm = (columns // frame_cols).astype(jnp.float32) / frame_rows
    cols_norm = (columns % frame_cols).astype(jnp.float32) / frame_cols
    return jnp.stack([rows_norm, cols_norm, jnp.ones_like(rows_norm)], axis=1)

def reference(source_feats, target_feats, back_flow, attn_weights, norm_gain, fetch_list, dest_local):
    half_window = WIN // 2
    feats_one = window_section(source_feats, None, attn_weights[0], norm_gain[0])
    rolled = jnp.roll(feats_one, (-half_window, -half_window), axis=(0, 1))
    row_ids = (jnp.arange(HQ, dtype=jnp.int32) + half_window) % HQ
    col_ids = (jnp.arange(WQ, dtype=jnp.int32) + half_window) % WQ
    region = (row_ids < half_window).astype(jnp.int32)[:, None] * 2 + (col_ids < half_window).astype(jnp.int32)[None, :]
    feats_two = jnp.roll(window_section(rolled, region, attn_weights[1], norm_gain[1]), (half_window, half_window), axis=(0, 1))
    blocks = N_PB * N_TA
    per_block = TQH * TQW
    query_blocks = feats_two.reshape(N_PB, TQH, N_TA, TQW, C).transpose(0, 2, 1, 3, 4).reshape(blocks, per_block, C)
    dest_blocks = dest_local.reshape(N_PB, TQH, N_TA, TQW).transpose(0, 2, 1, 3).reshape(blocks, per_block)
    coord_rows = coord_table(jnp.arange(NT, dtype=jnp.int32), HQ, WQ)
    local_ids = jnp.arange(per_block, dtype=jnp.int32)

    def one_block(packed):
        queries, block_id, fetch_row, dest_row = packed
        scores = jnp.dot(queries, target_feats, preferred_element_type=jnp.float32) * (MATCH_GAIN / math.sqrt(C))
        highest = lax.optimization_barrier(jnp.max(scores, axis=1, keepdims=True))
        raised = jnp.exp(scores - highest)
        totals = jnp.dot(raised, coord_rows, precision=lax.Precision.HIGHEST)
        query_rows = (block_id // N_TA * TQH + local_ids // TQW).astype(jnp.float32) / HQ
        query_cols = (block_id % N_TA * TQW + local_ids % TQW).astype(jnp.float32) / WQ
        flow_rows = totals[:, 0] / totals[:, 2] - query_rows
        flow_cols = totals[:, 1] / totals[:, 2] - query_cols
        target_ids = (fetch_row[dest_row // TB] * TB + dest_row % TB).astype(jnp.int32)
        backward = back_flow[:, target_ids].astype(jnp.float32)
        diff_sq = (flow_rows + backward[0]) ** 2 + (flow_cols + backward[1]) ** 2
        magnitude = flow_rows ** 2 + flow_cols ** 2 + backward[0] ** 2 + backward[1] ** 2
        consistency = jnp.exp(-diff_sq / (FLOW_ALPHA * magnitude + FLOW_BETA))
        return jnp.stack([flow_rows, flow_cols, consistency])
    results = lax.map(one_block, (query_blocks, jnp.arange(blocks, dtype=jnp.int32), fetch_list, dest_blocks))
    results = results.reshape(N_PB, N_TA, 3, TQH, TQW).transpose(2, 0, 3, 1, 4).reshape(3, HQ, WQ)
    return (results[:2], results[2])
```

```python
import math

import jax
import jax.numpy as jnp
from jax import lax
from jax.experimental import pallas as pl
from jax.experimental.pallas import tpu as pltpu
from jax.sharding import PartitionSpec as P

MESH = pl.DeviceIdType.MESH
NORM_EPSILON = 1e-05
MATCH_GAIN = 2.0
FLOW_ALPHA = 0.01
FLOW_BETA = 0.5
CH = 128
PB, TA = 4, 64
NX, NZ = 4, 8
FRAME_ROWS, FRAME_COLS = 128, 512
TILE_ROWS, TILE_COLS = 32, 8
PIXELS = TILE_ROWS * TILE_COLS
SLOTS = 8
CHUNKS, CHUNK_COLS = 16, 32
NEG = -1e30
SCORE_LOG2 = MATCH_GAIN / math.sqrt(CH) * math.log2(math.e)


def tree_sum(xs):
    xs = list(xs)
    while len(xs) > 1:
        xs = [xs[i] + xs[i + 1] for i in range(0, len(xs), 2)]
    return xs[0]


def weighted_tree(xs, weights):
    odd, cur = [], list(xs)
    while len(cur) > 1:
        odd.append(tree_sum(cur[1::2]))
        cur = [cur[i] + cur[i + 1] for i in range(0, len(cur), 2)]
    total = None
    for value, weight in zip(odd, weights):
        term = value * float(weight)
        total = term if total is None else total + term
    return cur[0], total


def normed(message, gain):
    center = message - jnp.mean(message, axis=-1, keepdims=True)
    spread = jnp.mean(center * center, axis=-1, keepdims=True)
    return center * lax.rsqrt(spread + NORM_EPSILON) * gain


def attend(queries, keys, values, admitted):
    scores = lax.dot_general(
        queries, keys, (((1,), (1,)), ((), ())), preferred_element_type=jnp.float32
    ) * (1.0 / math.sqrt(CH))
    scores = jnp.where(admitted, scores, NEG)
    raised = jnp.exp(scores - jnp.max(scores, axis=-1, keepdims=True))
    weights = (raised / jnp.sum(raised, axis=-1, keepdims=True)).astype(jnp.bfloat16)
    return jnp.dot(weights, values, preferred_element_type=jnp.float32).astype(jnp.bfloat16)


def project(pixels, matrix):
    return jnp.dot(pixels, matrix, preferred_element_type=jnp.float32).astype(jnp.bfloat16)


def iota(shape, axis):
    return lax.broadcasted_iota(jnp.int32, shape, axis)


def place():
    pb, ta = lax.axis_index("pb"), lax.axis_index("ta")
    yh, z, x = lax.div(ta, 32), lax.rem(lax.div(ta, NX), NZ), lax.rem(ta, NX)
    return pb, ta, yh, z, x


def target_peer(pb, z, slot):
    return (pb, lax.div(slot, NX) * 32 + z * NX + lax.rem(slot, NX))


def kernel(
    src_ref, tgt_ref, back_ref, w_ref, gain_ref, dest_ref, out_ref,
    tset, bset, dset, qset, halo, res, rset,
    t_send, t_recv, f_send, f_recv, b_send, b_recv, d_send, d_recv,
    q_send, q_recv, r_send, r_recv, h_send, h_recv,
):
    pb, ta, yh, z, x = place()
    core = lax.rem(pb, 2)
    mate = (pb + 1 - 2 * core, ta)
    slot = yh * NX + x
    up, down = lax.rem(pb + PB - 1, PB), lax.rem(pb + 1, PB)
    left, right = lax.rem(ta + TA - 1, TA), lax.rem(ta + 1, TA)

    def z_peer(offset):
        return (pb, yh * 32 + lax.rem(z + offset + NZ, NZ) * NX + x)

    def remote(src, dst, send, recv, device):
        return pltpu.make_async_remote_copy(
            src_ref=src, dst_ref=dst, send_sem=send, recv_sem=recv, device_id=device, device_id_type=MESH
        )

    halo_copies = [
        remote(halo.at[:, 16:32], halo.at[:, 144:160], h_send.at[0], h_recv.at[0], (up, ta)),
        remote(halo.at[:, 128:144], halo.at[:, 0:16], h_send.at[1], h_recv.at[1], (down, ta)),
        remote(halo.at[1, 16:144], halo.at[0, 176:304], h_send.at[2], h_recv.at[2], (pb, right)),
        remote(halo.at[0, 16:144], halo.at[1, 176:304], h_send.at[3], h_recv.at[3], (pb, left)),
        remote(halo.at[1, 16:32], halo.at[0, 304:320], h_send.at[4], h_recv.at[4], (up, right)),
        remote(halo.at[1, 128:144], halo.at[0, 160:176], h_send.at[5], h_recv.at[5], (down, right)),
        remote(halo.at[0, 16:32], halo.at[1, 304:320], h_send.at[6], h_recv.at[6], (up, left)),
        remote(halo.at[0, 128:144], halo.at[1, 160:176], h_send.at[7], h_recv.at[7], (down, left)),
    ]

    barrier = pltpu.get_barrier_semaphore()
    for device in (
        (up, ta), (down, ta), (pb, right), (pb, left), (up, right), (down, right), (up, left), (down, left), mate,
    ):
        pl.semaphore_signal(barrier, inc=1, device_id=device, device_id_type=MESH)

    def greet(d, carry):
        pl.semaphore_signal(
            barrier, inc=1, device_id=target_peer(pb, z, lax.rem(slot + d, SLOTS)), device_id_type=MESH
        )
        pl.semaphore_signal(barrier, inc=1, device_id=z_peer(d), device_id_type=MESH)
        return carry

    lax.fori_loop(1, SLOTS, greet, 0)

    turned = tgt_ref[...].T
    for g in range(CHUNKS):
        for r in range(2):
            at = r * FRAME_COLS + g * CHUNK_COLS
            tset[slot, g, r * CHUNK_COLS : (r + 1) * CHUNK_COLS] = turned[at : at + CHUNK_COLS]
    bset[slot] = back_ref[...]
    dset[0] = dest_ref[...]

    pl.semaphore_wait(barrier, 9 + 2 * (SLOTS - 1))

    half = pl.ds(core * (CHUNKS // 2), CHUNKS // 2)

    def target_copy(s, device):
        return remote(tset.at[s, half], tset.at[s, half], t_send.at[lax.rem(s + 0, SLOTS)], t_recv.at[s], device)

    def share_target(d, carry):
        other = lax.rem(slot + d, SLOTS)
        device = target_peer(pb, z, other)
        remote(tset.at[slot, half], tset.at[slot, half], t_send.at[d], t_recv.at[slot], device).start()
        remote(bset.at[slot], bset.at[slot], b_send.at[d], b_recv.at[slot], device).start()
        remote(dset.at[0], dset.at[d], d_send.at[d], d_recv.at[d], z_peer(d)).start()
        return carry

    i = iota((PIXELS, PIXELS), 0)
    j = iota((PIXELS, PIXELS), 1)
    wanted = ((i >> 2) & 31) * 8 + (i >> 7) * 4 + (i & 3)
    order = jnp.where(wanted == j, 1.0, 0.0).astype(jnp.bfloat16)
    pixels = project(order, src_ref[...])
    same = ((i >> 5) & 3) == ((j >> 5) & 3)
    attended = attend(
        project(pixels, w_ref[0, 0]), project(pixels, w_ref[0, 1]), project(pixels, w_ref[0, 2]), same
    )
    message = jnp.dot(attended, w_ref[0, 3], preferred_element_type=jnp.float32)
    one = (pixels.astype(jnp.float32) + normed(message, gain_ref[0:1])).astype(jnp.bfloat16)
    halo[0, 16:144] = one[:128]
    halo[1, 16:144] = one[128:]
    for copy in halo_copies:
        copy.start()
    lax.fori_loop(1, SLOTS, share_target, 0)
    for copy in halo_copies:
        copy.wait()

    i = iota((128, 320), 0)
    j = iota((128, 320), 1)
    beside = j >= 160
    kk = jnp.where(beside, j - 160, j)
    row, key_row = i >> 2, (kk >> 2) - 4
    low = pb * TILE_ROWS + row < 4
    key_low = ((pb * TILE_ROWS + key_row + FRAME_ROWS) & (FRAME_ROWS - 1)) < 4
    rows_agree = (((row + 4) >> 3) == (kk >> 5)) & (low == key_low)
    for h, edge in ((0, 0), (1, TA - 1)):
        admitted = rows_agree & jnp.logical_not(beside & (ta == edge))
        around = halo[h]
        own = halo[h, 16:144]
        attended = attend(
            project(own, w_ref[1, 0]), project(around, w_ref[1, 1]), project(around, w_ref[1, 2]), admitted
        )
        message = jnp.dot(attended, w_ref[1, 3], preferred_element_type=jnp.float32)
        two = (own.astype(jnp.float32) + normed(message, gain_ref[1:2])).astype(jnp.bfloat16)
        qset[0, h * 128 : (h + 1) * 128] = (two.astype(jnp.float32) * SCORE_LOG2).astype(jnp.bfloat16)

    def nth(k):
        odd = lax.rem(k, 2)
        return lax.rem(odd * lax.div(k + 1, 2) + (1 - odd) * (NZ - lax.div(k, 2)), NZ)

    def query_copy(o):
        return remote(qset.at[0], qset.at[o], q_send.at[o], q_recv.at[o], z_peer(o))

    def share_queries(k, carry):
        query_copy(nth(k)).start()
        return carry

    lax.fori_loop(1, SLOTS, share_queries, 0)

    def forward_target(d, carry):
        other = lax.rem(slot + d, SLOTS)
        part = tset.at[other, half]
        remote(part, part, t_send.at[d], t_recv.at[other], mate).wait_recv()
        remote(part, part, f_send.at[d], f_recv.at[other], mate).start()
        return carry

    lax.fori_loop(1, SLOTS, forward_target, 0)

    def land_forwards(d, carry):
        other = lax.rem(slot + d, SLOTS)
        part = tset.at[other, pl.ds((1 - core) * (CHUNKS // 2), CHUNKS // 2)]
        remote(part, part, f_send.at[d], f_recv.at[other], mate).wait_recv()
        remote(bset.at[other], bset.at[other], b_send.at[d], b_recv.at[other], mate).wait_recv()
        return carry

    sub = iota((8, PIXELS), 0).astype(jnp.float32)

    def match_chunk(g, state, queries):
        top, s0, s1, s2 = state
        feats = tset[:, pl.ds(g, 1)].reshape(SLOTS * 2 * CHUNK_COLS, CH)
        scores = lax.dot_general(
            feats, queries, (((1,), (1,)), ((), ())), preferred_element_type=jnp.float32
        ).reshape(2 * SLOTS, CHUNK_COLS // 8, 8, PIXELS)
        new_top = jnp.maximum(top, jnp.max(scores, axis=(0, 1)))
        fade = jnp.exp2(top - new_top)
        raised = jnp.exp2(scores - new_top[None, None])
        by_col = [tree_sum([raised[r, c] for r in range(16)]) for c in range(4)]
        by_row = [tree_sum([raised[r, c] for c in range(4)]) for r in range(16)]
        _, row_part = weighted_tree(by_row, (1, 2, 4, 64))
        total, col_part = weighted_tree(by_col, (8, 16))
        col_part = col_part + total * (sub + (g * CHUNK_COLS).astype(jnp.float32))
        return new_top, s0 * fade + row_part, s1 * fade + col_part, s2 * fade + total

    def match_block(k, carry):
        o = nth(k)

        @pl.when(k > 0)
        def _():
            query_copy(o).wait_recv()
            remote(dset.at[0], dset.at[o], d_send.at[o], d_recv.at[o], z_peer(o)).wait_recv()

        queries = qset[o]
        zero = jnp.zeros((8, PIXELS), jnp.float32)
        state = (zero + NEG, zero, zero, zero)
        state = lax.fori_loop(
            0, CHUNKS // 2, lambda g, s: match_chunk(core * (CHUNKS // 2) + g, s, queries), state, unroll=8
        )

        @pl.when(k == 0)
        def _():
            lax.fori_loop(1, SLOTS, land_forwards, 0)

        top, s0, s1, s2 = lax.fori_loop(
            0, CHUNKS // 2, lambda g, s: match_chunk((1 - core) * (CHUNKS // 2) + g, s, queries), state, unroll=8
        )
        best = jnp.max(top, axis=0, keepdims=True)
        scale = jnp.exp2(top - best)
        t2 = jnp.sum(s2 * scale, axis=0, keepdims=True)
        t0 = jnp.sum(s0 * scale, axis=0, keepdims=True) + t2 * (z * 8).astype(jnp.float32)
        t1 = jnp.sum(s1 * scale, axis=0, keepdims=True)

        dest = dset[o][0:1]
        block, off = dest >> 10, dest & 1023
        here = ((block >> 2) & 7) == z
        at = jnp.where(here, ((block >> 5) * NX + (block & 3)) * 16 + (off >> 7), -1000)
        lanes = jnp.where(iota((CH, PIXELS), 0) == (off & 127), 1.0, 0.0).astype(jnp.bfloat16)
        picked = jnp.dot(bset[...].reshape(SLOTS * 16, CH), lanes, preferred_element_type=jnp.float32)
        line = iota((SLOTS * 16, PIXELS), 0)
        back0 = jnp.sum(jnp.where(line == at, picked, 0.0), axis=0, keepdims=True)
        back1 = jnp.sum(jnp.where(line == at + 8, picked, 0.0), axis=0, keepdims=True)
        pad = jnp.zeros((2, PIXELS), jnp.float32)
        res[k] = jnp.concatenate([best, t0, t1, t2, back0, back1, pad], axis=0)

        @pl.when(k > 0)
        def _():
            remote(res.at[k], rset.at[o], r_send.at[k], r_recv.at[o], z_peer(-o)).start()

        return carry

    lax.fori_loop(0, SLOTS, match_block, 0)

    def settle(d, carry):
        remote(res.at[d], rset.at[d], r_send.at[d], r_recv.at[d], mate).wait_recv()
        return carry

    lax.fori_loop(1, SLOTS, settle, 0)
    parts = [res[0]] + [rset[o] for o in range(1, SLOTS)]
    best = parts[0]
    for part in parts[1:]:
        best = jnp.maximum(best, part)
    best = best[0:1]
    total = jnp.zeros((8, PIXELS), jnp.float32)
    back = jnp.zeros((8, PIXELS), jnp.float32)
    for part in parts:
        total = total + part * jnp.exp2(part[0:1] - best)
        back = back + part
    p = iota((1, PIXELS), 1)
    row = (pb * TILE_ROWS + ((p >> 2) & 31)).astype(jnp.float32) / FRAME_ROWS
    col = (ta * TILE_COLS + (p >> 7) * 4 + (p & 3)).astype(jnp.float32) / FRAME_COLS
    flow0 = total[1:2] / total[3:4] / FRAME_ROWS - row
    flow1 = total[2:3] / total[3:4] / FRAME_COLS - col
    back0, back1 = back[4:5], back[5:6]
    diff = (flow0 + back0) ** 2 + (flow1 + back1) ** 2
    mag = flow0**2 + flow1**2 + back0**2 + back1**2
    cons = jnp.exp(-diff / (FLOW_ALPHA * mag + FLOW_BETA))
    out_ref[...] = jnp.concatenate([flow0, flow1, cons, jnp.zeros((5, PIXELS), jnp.float32)], axis=0)

    def finish(d, carry):
        part = tset.at[slot, half]
        remote(part, part, t_send.at[d], t_recv.at[slot], mate).wait_send()
        remote(part, part, f_send.at[d], f_recv.at[slot], mate).wait_send()
        remote(bset.at[slot], bset.at[slot], b_send.at[d], b_recv.at[slot], mate).wait_send()
        remote(dset.at[0], dset.at[d], d_send.at[d], d_recv.at[d], mate).wait_send()
        query_copy(d).wait_send()
        remote(res.at[d], rset.at[d], r_send.at[d], r_recv.at[d], mate).wait_send()
        return carry

    lax.fori_loop(1, SLOTS, finish, 0)


def shards(source_feats, target_feats, back_flow, attn_weights, norm_gain, fetch_list, dest_local):
    slots = dest_local >> 10
    block = jnp.zeros_like(dest_local)
    for k in range(fetch_list.shape[1]):
        block = jnp.where(slots == k, fetch_list[0, k], block)
    dest = block * 1024 + (dest_local & 1023)
    dest = dest.reshape(TILE_ROWS, 2, 4).transpose(1, 0, 2).reshape(1, PIXELS)
    dest = jnp.broadcast_to(dest, (8, PIXELS))
    vmem = pl.BlockSpec(memory_space=pltpu.VMEM)
    dma = pltpu.SemaphoreType.DMA((SLOTS,))
    out = pl.pallas_call(
        kernel,
        out_shape=jax.ShapeDtypeStruct((8, PIXELS), jnp.float32),
        in_specs=[vmem] * 6,
        out_specs=vmem,
        scratch_shapes=[
            pltpu.VMEM((SLOTS, CHUNKS, 2 * CHUNK_COLS, CH), jnp.bfloat16),
            pltpu.VMEM((SLOTS, 16, CH), jnp.bfloat16),
            pltpu.VMEM((SLOTS, 8, PIXELS), jnp.int32),
            pltpu.VMEM((SLOTS, PIXELS, CH), jnp.bfloat16),
            pltpu.VMEM((2, 320, CH), jnp.bfloat16),
            pltpu.VMEM((SLOTS, 8, PIXELS), jnp.float32),
            pltpu.VMEM((SLOTS, 8, PIXELS), jnp.float32),
        ]
        + [dma] * 14,
        compiler_params=pltpu.CompilerParams(
            collective_id=0, has_side_effects=True, vmem_limit_bytes=40 << 20
        ),
    )(
        source_feats.reshape(PIXELS, CH),
        target_feats,
        back_flow.reshape(16, CH),
        attn_weights,
        norm_gain,
        dest,
    )
    out = out[:3].reshape(3, 2, TILE_ROWS, 4).transpose(0, 2, 1, 3).reshape(3, TILE_ROWS, TILE_COLS)
    return out[:2], out[2]


def solution(mesh):
    placed = (
        P("pb", "ta", None),
        P(None, "ta"),
        P(None, "ta"),
        P(),
        P(),
        P(("pb", "ta"), None),
        P("pb", "ta"),
    )
    return jax.shard_map(
        shards,
        mesh=mesh,
        in_specs=placed,
        out_specs=(P(None, "pb", "ta"), P("pb", "ta")),
        check_vma=False,
    )
```

```python
import math

import jax
import jax.numpy as jnp
from jax import lax
from jax.experimental import pallas as pl
from jax.experimental.pallas import tpu as pltpu
from jax.sharding import PartitionSpec as P

MESH = pl.DeviceIdType.MESH
NORM_EPSILON = 1e-05
MATCH_GAIN = 2.0
FLOW_ALPHA = 0.01
FLOW_BETA = 0.5
CH = 128
PB, TA = 4, 64
NX, NZ = 4, 8
FRAME_ROWS, FRAME_COLS = 128, 512
TILE_ROWS, TILE_COLS = 32, 8
PIXELS = TILE_ROWS * TILE_COLS
BLOCKS = NZ
GROUP = 4
ROW_STEP = 2 * GROUP
ORIGINS = ((0, 0), (0, 1), (0, 3), (1, 0), (0, 2), (1, 1), (1, 3), (1, 2))
HOPS = ((0, 1, 0, 1), (0, 2, 0, -1), (0, 3, 1, 0), (2, 4, 0, -1), (3, 5, 0, 1), (3, 6, 0, -1), (3, 7, 0, 2))
CHUNKS, CHUNK_COLS = 8, 64
NEG = -1e30
SCORE_LOG2 = MATCH_GAIN / math.sqrt(CH) * math.log2(math.e)


def tree_sum(xs):
    xs = list(xs)
    while len(xs) > 1:
        xs = [xs[i] + xs[i + 1] for i in range(0, len(xs), 2)]
    return xs[0]


def weighted_tree(xs, weights):
    odd, cur = [], list(xs)
    while len(cur) > 1:
        odd.append(tree_sum(cur[1::2]))
        cur = [cur[i] + cur[i + 1] for i in range(0, len(cur), 2)]
    total = None
    for value, weight in zip(odd, weights):
        term = value * float(weight)
        total = term if total is None else total + term
    return cur[0], total


def normed(message, gain):
    center = message - jnp.mean(message, axis=-1, keepdims=True)
    spread = jnp.mean(center * center, axis=-1, keepdims=True)
    return center * lax.rsqrt(spread + NORM_EPSILON) * gain


def attend(queries, keys, values, admitted):
    scores = lax.dot_general(
        queries, keys, (((1,), (1,)), ((), ())), preferred_element_type=jnp.float32
    ) * (1.0 / math.sqrt(CH))
    scores = jnp.where(admitted, scores, NEG)
    raised = jnp.exp(scores - jnp.max(scores, axis=-1, keepdims=True))
    weights = (raised / jnp.sum(raised, axis=-1, keepdims=True)).astype(jnp.bfloat16)
    return jnp.dot(weights, values, preferred_element_type=jnp.float32).astype(jnp.bfloat16)


def project(pixels, matrix):
    return jnp.dot(pixels, matrix, preferred_element_type=jnp.float32).astype(jnp.bfloat16)


def iota(shape, axis):
    return lax.broadcasted_iota(jnp.int32, shape, axis)


def place():
    pb, ta = lax.axis_index("pb"), lax.axis_index("ta")
    yh, z, x = lax.div(ta, 32), lax.rem(lax.div(ta, NX), NZ), lax.rem(ta, NX)
    return pb, ta, yh, z, x


def kernel(
    src_hbm, tgt_hbm, back_hbm, w_hbm, gain_hbm, fetch_hbm, dest_hbm, flow_ref, cons_ref,
    src_ref, tgt_ref, back_ref, w_ref, gain_ref, fetch_ref, dest_ref, load_sem,
    tset, bset, qset, halo, res, rset, state, first_top, even, odd,
    t_send, t_recv, f_send, f_recv, b_send, b_recv,
    q_send, q_recv, r_send, r_recv, h_send, h_recv,
):
    pb, ta, yh, z, x = place()
    core = lax.rem(pb, 2)
    mate = (pb + 1 - 2 * core, ta)
    up, down = lax.rem(pb + PB - 1, PB), lax.rem(pb + 1, PB)
    left, right = lax.rem(ta + TA - 1, TA), lax.rem(ta + 1, TA)

    def z_peer(offset):
        return (pb, yh * 32 + lax.rem(z + offset + NZ, NZ) * NX + x)

    def x_peer(side, offset):
        far = core + 2 * (1 - lax.div(pb, 2))
        half = yh + side - 2 * yh * side
        return (pb + side * (far - pb), half * 32 + z * NX + lax.rem(x + offset + NX, NX))

    def remote(src, dst, send, recv, device):
        return pltpu.make_async_remote_copy(
            src_ref=src, dst_ref=dst, send_sem=send, recv_sem=recv, device_id=device, device_id_type=MESH
        )

    halo_copies = [
        remote(halo.at[:, 16:32], halo.at[:, 144:160], h_send.at[0], h_recv.at[0], (up, ta)),
        remote(halo.at[:, 128:144], halo.at[:, 0:16], h_send.at[1], h_recv.at[1], (down, ta)),
        remote(halo.at[1, 16:144], halo.at[0, 176:304], h_send.at[2], h_recv.at[2], (pb, right)),
        remote(halo.at[0, 16:144], halo.at[1, 176:304], h_send.at[3], h_recv.at[3], (pb, left)),
        remote(halo.at[1, 16:32], halo.at[0, 304:320], h_send.at[4], h_recv.at[4], (up, right)),
        remote(halo.at[1, 128:144], halo.at[0, 160:176], h_send.at[5], h_recv.at[5], (down, right)),
        remote(halo.at[0, 16:32], halo.at[1, 304:320], h_send.at[6], h_recv.at[6], (up, left)),
        remote(halo.at[0, 128:144], halo.at[1, 160:176], h_send.at[7], h_recv.at[7], (down, left)),
    ]

    loads = [
        pltpu.make_async_copy(a, b, load_sem.at[n])
        for n, (a, b) in enumerate(
            (
                (tgt_hbm, tgt_ref), (back_hbm, back_ref), (src_hbm, src_ref), (w_hbm, w_ref),
                (gain_hbm, gain_ref), (fetch_hbm, fetch_ref), (dest_hbm, dest_ref),
            )
        )
    ]
    for copy in loads:
        copy.start()

    barrier = pltpu.get_barrier_semaphore()
    for device in (
        (up, ta), (down, ta), (pb, right), (pb, left), (up, right), (down, right), (up, left), (down, left), mate,
        x_peer(0, 1), x_peer(0, 2), x_peer(0, 3), x_peer(1, 0),
    ):
        pl.semaphore_signal(barrier, inc=1, device_id=device, device_id_type=MESH)

    def greet(o, carry):
        pl.semaphore_signal(barrier, inc=1, device_id=z_peer(o), device_id_type=MESH)
        return carry

    lax.fori_loop(1, NZ, greet, 0)

    half = pl.ds(core * (CHUNKS // 2), CHUNKS // 2)
    other_half = pl.ds((1 - core) * (CHUNKS // 2), CHUNKS // 2)

    def block_copy(n):
        held, rank, side, steps = HOPS[n]
        return remote(tset.at[held, half], tset.at[rank, half], t_send.at[n], t_recv.at[rank], x_peer(side, steps))

    def back_copy(n):
        held, rank, side, steps = HOPS[n]
        return remote(bset.at[held], bset.at[rank], b_send.at[n], b_recv.at[rank], x_peer(side, steps))

    def mate_copy(rank, part):
        return remote(tset.at[rank, part], tset.at[rank, part], f_send.at[rank], f_recv.at[rank], mate)

    def pass_on(n):
        block_copy(n).start()
        back_copy(n).start()

    def take(n):
        block_copy(n).wait_recv()
        back_copy(n).wait_recv()
        mate_copy(HOPS[n][1], half).start()

    for copy in loads[:2]:
        copy.wait()
    turned = tgt_ref[...].T
    for g in range(CHUNKS):
        for r in range(2):
            at = r * FRAME_COLS + g * CHUNK_COLS
            tset[0, g, r * CHUNK_COLS : (r + 1) * CHUNK_COLS] = turned[at : at + CHUNK_COLS]
    back = back_ref[...].astype(jnp.float32)
    bset[0] = jnp.concatenate([back[:, CH * n : CH * n + CH] for n in range(8)], axis=0).astype(jnp.bfloat16)
    pl.semaphore_wait(barrier, 13 + (BLOCKS - 1))
    for n in (0, 1, 2):
        pass_on(n)
    for copy in loads[2:]:
        copy.wait()
    picks = dest_ref[...]
    listed = jnp.zeros_like(picks)
    for n in range(4):
        listed = jnp.where((picks >> 10) == n, fetch_ref[0:1, n : n + 1], listed)
    dests = listed * 1024 + (picks & 1023)
    pixel = iota((TILE_ROWS, PIXELS), 1)
    row_of = ((pixel >> 2) & 31) == iota((TILE_ROWS, PIXELS), 0)
    row_hot = jnp.where(row_of, 1.0, 0.0).astype(jnp.bfloat16)
    pixel = iota((TILE_COLS, PIXELS), 1)
    col_of = (pixel >> 7) * 4 + (pixel & 3) == iota((TILE_COLS, PIXELS), 0)
    spread = [
        jnp.dot(part.astype(jnp.float32).astype(jnp.bfloat16), row_hot, preferred_element_type=jnp.float32)
        for part in (dests >> 8, dests & 255)
    ]
    spread = jnp.where(col_of, spread[0] * 256.0 + spread[1], 0.0)
    spread = jnp.sum(spread, axis=0, keepdims=True)
    coarse = jnp.floor(spread * (1.0 / 256.0))
    pair = jnp.concatenate([coarse, spread - coarse * 256.0], axis=0)
    qset[0, PIXELS:] = jnp.concatenate(
        [pair[:, :CH], pair[:, CH:], jnp.zeros((12, CH), jnp.float32)], axis=0
    ).astype(jnp.bfloat16)

    i = iota((PIXELS, PIXELS), 0)
    j = iota((PIXELS, PIXELS), 1)
    wanted = ((i >> 2) & 31) * 8 + (i >> 7) * 4 + (i & 3)
    order = jnp.where(wanted == j, 1.0, 0.0).astype(jnp.bfloat16)
    pixels = project(order, src_ref[...])
    same = ((i >> 5) & 3) == ((j >> 5) & 3)
    attended = attend(
        project(pixels, w_ref[0, 0]), project(pixels, w_ref[0, 1]), project(pixels, w_ref[0, 2]), same
    )
    message = jnp.dot(attended, w_ref[0, 3], preferred_element_type=jnp.float32)
    one = (pixels.astype(jnp.float32) + normed(message, gain_ref[0:1])).astype(jnp.bfloat16)
    halo[0, 16:144] = one[:128]
    halo[1, 16:144] = one[128:]
    for copy in halo_copies:
        copy.start()
    for copy in halo_copies:
        copy.wait()

    i = iota((128, 320), 0)
    j = iota((128, 320), 1)
    beside = j >= 160
    kk = jnp.where(beside, j - 160, j)
    row, key_row = i >> 2, (kk >> 2) - 4
    low = pb * TILE_ROWS + row < 4
    key_low = ((pb * TILE_ROWS + key_row + FRAME_ROWS) & (FRAME_ROWS - 1)) < 4
    rows_agree = (((row + 4) >> 3) == (kk >> 5)) & (low == key_low)
    for h, edge in ((0, 0), (1, TA - 1)):
        admitted = rows_agree & jnp.logical_not(beside & (ta == edge))
        around = halo[h]
        own = halo[h, 16:144]
        attended = attend(
            project(own, w_ref[1, 0]), project(around, w_ref[1, 1]), project(around, w_ref[1, 2]), admitted
        )
        message = jnp.dot(attended, w_ref[1, 3], preferred_element_type=jnp.float32)
        two = (own.astype(jnp.float32) + normed(message, gain_ref[1:2])).astype(jnp.bfloat16)
        qset[0, h * 128 : (h + 1) * 128] = (two.astype(jnp.float32) * SCORE_LOG2).astype(jnp.bfloat16)

    def nth(k):
        odd = lax.rem(k, 2)
        return lax.rem(odd * lax.div(k + 1, 2) + (1 - odd) * (NZ - lax.div(k, 2)), NZ)

    def query_copy(o):
        return remote(qset.at[0], qset.at[o], q_send.at[o], q_recv.at[o], z_peer(o))

    def result_copy(o):
        return remote(res.at[o], rset.at[o], r_send.at[o], r_recv.at[o], z_peer(-o))

    query_copy(1).start()
    query_copy(7).start()
    take(0)
    take(1)
    pass_on(3)
    take(2)
    for n in (4, 5, 6):
        pass_on(n)
    for rank in (1, 2, 3):
        mate_copy(rank, other_half).wait_recv()

    sub = iota((8, PIXELS), 0).astype(jnp.float32)
    origins = [(yh + side - 2 * yh * side, lax.rem(x + NX - o, NX)) for side, o in ORIGINS]
    base = (z * 8).astype(jnp.float32)
    row_weights = [(half_of * 64 + column * 2).astype(jnp.float32) for half_of, column in origins]

    def score_chunk(g, late, queries, buffer, top):
        feats = tset[pl.ds(late * GROUP, GROUP), g].reshape(ROW_STEP * CHUNK_COLS, CH)
        scores = lax.dot_general(
            feats, queries, (((1,), (1,)), ((), ())), preferred_element_type=jnp.float32
        )
        buffer[...] = scores
        return jnp.maximum(top, jnp.max(scores.reshape(-1, 8, PIXELS), axis=0))

    def sum_chunk(g, weights, buffer, top, new_top, sums):
        s0, s1, s2 = sums
        fade = jnp.exp2(top - new_top)
        scores = buffer[...].reshape(ROW_STEP, CHUNK_COLS // 8, 8, PIXELS)
        raised = jnp.exp2(scores - new_top[None, None])
        by_row = jnp.sum(raised, axis=1)
        by_col = jnp.sum(raised, axis=0)
        total, col_part = weighted_tree([by_col[n] for n in range(CHUNK_COLS // 8)], (8, 16, 32))
        row_part = tree_sum([by_row[2 * n + 1] for n in range(GROUP)]) + total * base
        for n in range(GROUP):
            row_part = row_part + (by_row[2 * n] + by_row[2 * n + 1]) * weights[n]
        col_part = col_part + total * (sub + float(g * CHUNK_COLS))
        return s0 * fade + row_part, s1 * fade + col_part, s2 * fade + total

    state[0] = jnp.zeros((4, 8, PIXELS), jnp.float32)
    res[0] = jnp.zeros((8, PIXELS), jnp.float32)
    floor = jnp.full((8, PIXELS), NEG, jnp.float32)
    buffers = (even, odd)

    def item(step):
        first, second = step < 5, step < 10
        late = jnp.where(first, 0, jnp.where(second, 1, lax.rem(step, 2)))
        k = jnp.where(first, step, jnp.where(second, step - 5, lax.div(step, 2)))
        return late, nth(k)

    def finish_block(o, late):
        top, s0, s1, s2 = tuple(state[o, m] for m in range(4))
        best = jnp.max(top, axis=0, keepdims=True)
        scale = jnp.exp2(top - best)
        t0 = jnp.sum(s0 * scale, axis=0, keepdims=True)
        t1 = jnp.sum(s1 * scale, axis=0, keepdims=True)
        t2 = jnp.sum(s2 * scale, axis=0, keepdims=True)

        marks = qset[o, PIXELS:].astype(jnp.float32)
        dest = jnp.concatenate(
            [marks[0:1] * 256.0 + marks[1:2], marks[2:3] * 256.0 + marks[3:4]], axis=1
        ).astype(jnp.int32)
        block, off = dest >> 10, dest & 1023
        here = ((block >> 2) & 7) == z
        at = jnp.zeros_like(block)
        for rank, (half_of, column) in enumerate(origins):
            at = jnp.where((block >> 5 == half_of) & ((block & 3) == column), rank * 16, at)
        at = jnp.where(here, at + (off >> 7) * 2, -1000) - late * (GROUP * 16)
        lanes = jnp.where(iota((CH, PIXELS), 0) == (off & 127), 1.0, 0.0).astype(jnp.bfloat16)
        table = bset[pl.ds(late * GROUP, GROUP)].reshape(GROUP * 16, CH)
        picked = jnp.dot(table, lanes, preferred_element_type=jnp.float32)
        line = iota((GROUP * 16, PIXELS), 0)
        back0 = jnp.sum(jnp.where(line == at, picked, 0.0), axis=0, keepdims=True)
        back1 = jnp.sum(jnp.where(line == at + 1, picked, 0.0), axis=0, keepdims=True)
        known = jnp.where(late == 1, res[o, 4:6], 0.0)
        back0, back1 = back0 + known[0:1], back1 + known[1:2]
        pad = jnp.zeros((2, PIXELS), jnp.float32)
        res[o] = jnp.concatenate([best, t0, t1, t2, back0, back1, pad], axis=0)

    def match_step(step, carry):
        late, o = item(step)
        before_late, before_o = item(jnp.maximum(step - 1, 0))
        alone = (step == 0) | (step == 4) | (step == 2 * BLOCKS - 1)
        next_late, next_o = item(jnp.where(alone, step, step + 1))

        @pl.when(step == 0)
        def _():
            query_copy(2).start()
            query_copy(6).start()

        @pl.when(step == 1)
        def _():
            query_copy(o).wait_recv()
            query_copy(3).start()
            query_copy(5).start()

        @pl.when(step == 3)
        def _():
            query_copy(4).start()

        @pl.when((next_late == 0) & jnp.logical_not(alone))
        def _():
            query_copy(next_o).wait_recv()

        @pl.when(step == 4)
        def _():
            for hop in (3, 4, 5, 6):
                take(hop)

        @pl.when(step == 5)
        def _():
            for rank in range(GROUP, BLOCKS):
                mate_copy(rank, other_half).wait_recv()

        queries, next_queries = qset[o, :PIXELS], qset[next_o, :PIXELS]

        @pl.when((step == 0) | (step == 1) | (step == 5))
        def _():
            first_top[...] = score_chunk(0, late, queries, even, floor)

        next_top = first_top[...]
        finish_block(before_o, before_late)
        weights = [jnp.where(late == 1, b, a) for a, b in zip(row_weights[:GROUP], row_weights[GROUP:])]
        top = jnp.where(late == 1, state[o, 0], floor)
        sums = tuple(jnp.where(late == 1, state[o, m], 0.0) for m in range(1, 4))
        next_top = jnp.maximum(next_top, top)
        for g in range(CHUNKS):
            last, top = top, next_top
            if g + 1 < CHUNKS:
                next_top = score_chunk(g + 1, late, queries, buffers[(g + 1) % 2], top)
            else:
                next_top = score_chunk(0, next_late, next_queries, even, floor)
            sums = sum_chunk(g, weights, buffers[g % 2], last, top, sums)
        state[o, 0] = top
        for m in range(3):
            state[o, m + 1] = sums[m]

        first_top[...] = next_top

        @pl.when((step > 0) & (before_late == 1) & (before_o > 0))
        def _():
            result_copy(before_o).start()

        return carry

    lax.fori_loop(0, 2 * BLOCKS, match_step, 0)
    finish_block(nth(BLOCKS - 1), 1)
    result_copy(nth(BLOCKS - 1)).start()

    def settle(n, carry):
        remote(res.at[n], rset.at[n], r_send.at[n], r_recv.at[n], mate).wait_recv()
        return carry

    lax.fori_loop(1, BLOCKS, settle, 0)
    parts = [res[0]] + [rset[n] for n in range(1, BLOCKS)]
    best = parts[0]
    for part in parts[1:]:
        best = jnp.maximum(best, part)
    best = best[0:1]
    total = jnp.zeros((8, PIXELS), jnp.float32)
    back = jnp.zeros((8, PIXELS), jnp.float32)
    for part in parts:
        total = total + part * jnp.exp2(part[0:1] - best)
        back = back + part
    p = iota((1, PIXELS), 1)
    row = (pb * TILE_ROWS + ((p >> 2) & 31)).astype(jnp.float32) / FRAME_ROWS
    col = (ta * TILE_COLS + (p >> 7) * 4 + (p & 3)).astype(jnp.float32) / FRAME_COLS
    flow0 = total[1:2] / total[3:4] / FRAME_ROWS - row
    flow1 = total[2:3] / total[3:4] / FRAME_COLS - col
    back0, back1 = back[4:5], back[5:6]
    diff = (flow0 + back0) ** 2 + (flow1 + back1) ** 2
    mag = flow0**2 + flow1**2 + back0**2 + back1**2
    cons = jnp.exp(-diff / (FLOW_ALPHA * mag + FLOW_BETA))
    moved = []
    for value in (flow0, flow1, cons):
        for _ in range(3):
            part = value.astype(jnp.bfloat16).astype(jnp.float32)
            moved.append(jnp.where(col_of, part, 0.0))
            value = value - part
    moved = lax.dot_general(
        jnp.concatenate(moved, axis=0).astype(jnp.bfloat16), row_hot, (((1,), (1,)), ((), ())),
        preferred_element_type=jnp.float32,
    )
    moved = [moved[n * TILE_COLS : (n + 1) * TILE_COLS] for n in range(9)]
    flow_ref[0] = moved[0] + moved[1] + moved[2]
    flow_ref[1] = moved[3] + moved[4] + moved[5]
    cons_ref[...] = moved[6] + moved[7] + moved[8]

    for n in range(NZ - 1):
        block_copy(n).wait_send()
        back_copy(n).wait_send()
        mate_copy(n + 1, half).wait_send()

    def finish(o, carry):
        query_copy(o).wait_send()
        result_copy(o).wait_send()
        return carry

    lax.fori_loop(1, BLOCKS, finish, 0)


def shards(source_feats, target_feats, back_flow, attn_weights, norm_gain, fetch_list, dest_local):
    vmem = pl.BlockSpec(memory_space=pltpu.VMEM)

    def dma(count):
        return pltpu.SemaphoreType.DMA((count,))

    args = (
        source_feats.reshape(PIXELS, CH), target_feats, back_flow, attn_weights, norm_gain, fetch_list, dest_local.T,
    )
    flow, cons = pl.pallas_call(
        kernel,
        out_shape=(
            jax.ShapeDtypeStruct((2, TILE_COLS, TILE_ROWS), jnp.float32),
            jax.ShapeDtypeStruct((TILE_COLS, TILE_ROWS), jnp.float32),
        ),
        in_specs=[pl.BlockSpec(memory_space=pl.ANY)] * len(args),
        out_specs=(vmem, vmem),
        scratch_shapes=[pltpu.VMEM(a.shape, a.dtype) for a in args]
        + [dma(len(args))]
        + [
            pltpu.VMEM((NZ, CHUNKS, 2 * CHUNK_COLS, CH), jnp.bfloat16),
            pltpu.VMEM((NZ, 16, CH), jnp.bfloat16),
            pltpu.VMEM((NZ, PIXELS + 16, CH), jnp.bfloat16),
            pltpu.VMEM((2, 320, CH), jnp.bfloat16),
            pltpu.VMEM((BLOCKS, 8, PIXELS), jnp.float32),
            pltpu.VMEM((BLOCKS, 8, PIXELS), jnp.float32),
            pltpu.VMEM((BLOCKS, 4, 8, PIXELS), jnp.float32),
            pltpu.VMEM((8, PIXELS), jnp.float32),
            pltpu.VMEM((ROW_STEP * CHUNK_COLS, PIXELS), jnp.float32),
            pltpu.VMEM((ROW_STEP * CHUNK_COLS, PIXELS), jnp.float32),
        ]
        + [dma(8)] * 12,
        compiler_params=pltpu.CompilerParams(
            collective_id=0, has_side_effects=True, vmem_limit_bytes=60 << 20
        ),
    )(*args)
    return jnp.swapaxes(flow, 1, 2), cons.T


def solution(mesh):
    placed = (
        P("pb", "ta", None),
        P(None, "ta"),
        P(None, "ta"),
        P(),
        P(),
        P(("pb", "ta"), None),
        P("pb", "ta"),
    )
    return jax.shard_map(
        shards,
        mesh=mesh,
        in_specs=placed,
        out_specs=(P(None, "pb", "ta"), P("pb", "ta")),
        check_vma=False,
    )
```

```python
import math

import jax
import jax.numpy as jnp
from jax import lax
from jax.experimental import pallas as pl
from jax.experimental.pallas import tpu as pltpu
from jax.sharding import PartitionSpec as P

MESH = pl.DeviceIdType.MESH
NORM_EPSILON = 1e-05
MATCH_GAIN = 2.0
FLOW_ALPHA = 0.01
FLOW_BETA = 0.5
CH = 128
PB, TA = 4, 64
NX, NZ = 4, 8
FRAME_ROWS, FRAME_COLS = 128, 512
TILE_ROWS, TILE_COLS = 32, 8
PIXELS = TILE_ROWS * TILE_COLS
BLOCKS = NZ
GROUP = 4
ROW_STEP = 2 * GROUP
ORIGINS = ((0, 0), (0, 1), (0, 3), (1, 0), (0, 2), (1, 1), (1, 3), (1, 2))
HOPS = ((0, 1, 0, 1), (0, 2, 0, -1), (0, 3, 1, 0), (2, 4, 0, -1), (1, 5, 1, 0), (2, 6, 1, 0), (3, 7, 0, 2))
CHUNKS, CHUNK_COLS = 8, 64
NEG = -1e30
SCORE_LOG2 = MATCH_GAIN / math.sqrt(CH) * math.log2(math.e)


def tree_sum(xs):
    xs = list(xs)
    while len(xs) > 1:
        xs = [xs[i] + xs[i + 1] for i in range(0, len(xs), 2)]
    return xs[0]


def weighted_tree(xs, weights):
    odd, cur = [], list(xs)
    while len(cur) > 1:
        odd.append(tree_sum(cur[1::2]))
        cur = [cur[i] + cur[i + 1] for i in range(0, len(cur), 2)]
    total = None
    for value, weight in zip(odd, weights):
        term = value * float(weight)
        total = term if total is None else total + term
    return cur[0], total


def normed(message, gain):
    center = message - jnp.mean(message, axis=-1, keepdims=True)
    spread = jnp.mean(center * center, axis=-1, keepdims=True)
    return center * lax.rsqrt(spread + NORM_EPSILON) * gain


def attend(queries, keys, values, admitted):
    scores = lax.dot_general(
        queries, keys, (((1,), (1,)), ((), ())), preferred_element_type=jnp.float32
    ) * (1.0 / math.sqrt(CH))
    scores = jnp.where(admitted, scores, NEG)
    raised = jnp.exp(scores - jnp.max(scores, axis=-1, keepdims=True))
    weights = (raised / jnp.sum(raised, axis=-1, keepdims=True)).astype(jnp.bfloat16)
    return jnp.dot(weights, values, preferred_element_type=jnp.float32).astype(jnp.bfloat16)


def project(pixels, matrix):
    return jnp.dot(pixels, matrix, preferred_element_type=jnp.float32).astype(jnp.bfloat16)


def iota(shape, axis):
    return lax.broadcasted_iota(jnp.int32, shape, axis)


def place():
    pb, ta = lax.axis_index("pb"), lax.axis_index("ta")
    yh, z, x = lax.div(ta, 32), lax.rem(lax.div(ta, NX), NZ), lax.rem(ta, NX)
    return pb, ta, yh, z, x


def kernel(
    src_hbm, tgt_hbm, back_hbm, w_hbm, gain_hbm, fetch_hbm, dest_hbm, flow_ref, cons_ref,
    src_ref, tgt_ref, back_ref, w_ref, gain_ref, fetch_ref, dest_ref, load_sem,
    tset, bset, qset, halo, res, rset, state, first_top, even, odd,
    t_send, t_recv, f_send, f_recv, b_send, b_recv,
    q_send, q_recv, r_send, r_recv, h_send, h_recv,
):
    pb, ta, yh, z, x = place()
    core = lax.rem(pb, 2)
    mate = (pb + 1 - 2 * core, ta)
    up, down = lax.rem(pb + PB - 1, PB), lax.rem(pb + 1, PB)
    left, right = lax.rem(ta + TA - 1, TA), lax.rem(ta + 1, TA)

    def z_peer(offset):
        return (pb, yh * 32 + lax.rem(z + offset + NZ, NZ) * NX + x)

    def x_peer(side, offset):
        far = core + 2 * (1 - lax.div(pb, 2))
        half = yh + side - 2 * yh * side
        return (pb + side * (far - pb), half * 32 + z * NX + lax.rem(x + offset + NX, NX))

    def remote(src, dst, send, recv, device):
        return pltpu.make_async_remote_copy(
            src_ref=src, dst_ref=dst, send_sem=send, recv_sem=recv, device_id=device, device_id_type=MESH
        )

    halo_copies = [
        remote(halo.at[:, 16:32], halo.at[:, 144:160], h_send.at[0], h_recv.at[0], (up, ta)),
        remote(halo.at[:, 128:144], halo.at[:, 0:16], h_send.at[1], h_recv.at[1], (down, ta)),
        remote(halo.at[1, 16:144], halo.at[0, 176:304], h_send.at[2], h_recv.at[2], (pb, right)),
        remote(halo.at[0, 16:144], halo.at[1, 176:304], h_send.at[3], h_recv.at[3], (pb, left)),
        remote(halo.at[1, 16:32], halo.at[0, 304:320], h_send.at[4], h_recv.at[4], (up, right)),
        remote(halo.at[1, 128:144], halo.at[0, 160:176], h_send.at[5], h_recv.at[5], (down, right)),
        remote(halo.at[0, 16:32], halo.at[1, 304:320], h_send.at[6], h_recv.at[6], (up, left)),
        remote(halo.at[0, 128:144], halo.at[1, 160:176], h_send.at[7], h_recv.at[7], (down, left)),
    ]

    loads = [
        pltpu.make_async_copy(a, b, load_sem.at[n])
        for n, (a, b) in enumerate(
            (
                (tgt_hbm, tgt_ref), (back_hbm, back_ref), (src_hbm, src_ref), (w_hbm, w_ref),
                (gain_hbm, gain_ref), (fetch_hbm, fetch_ref), (dest_hbm, dest_ref),
            )
        )
    ]
    for copy in loads:
        copy.start()

    barrier = pltpu.get_barrier_semaphore()
    for device in (
        (up, ta), (down, ta), (pb, right), (pb, left), (up, right), (down, right), (up, left), (down, left), mate,
        x_peer(0, 1), x_peer(0, 2), x_peer(0, 3), x_peer(1, 0),
    ):
        pl.semaphore_signal(barrier, inc=1, device_id=device, device_id_type=MESH)

    def greet(o, carry):
        pl.semaphore_signal(barrier, inc=1, device_id=z_peer(o), device_id_type=MESH)
        return carry

    lax.fori_loop(1, NZ, greet, 0)

    half = pl.ds(core * (CHUNKS // 2), CHUNKS // 2)
    other_half = pl.ds((1 - core) * (CHUNKS // 2), CHUNKS // 2)

    def block_copy(n):
        held, rank, side, steps = HOPS[n]
        return remote(tset.at[held, half], tset.at[rank, half], t_send.at[n], t_recv.at[rank], x_peer(side, steps))

    def back_copy(n):
        held, rank, side, steps = HOPS[n]
        return remote(bset.at[held], bset.at[rank], b_send.at[n], b_recv.at[rank], x_peer(side, steps))

    def mate_copy(rank, part):
        return remote(tset.at[rank, part], tset.at[rank, part], f_send.at[rank], f_recv.at[rank], mate)

    def pass_on(n):
        block_copy(n).start()
        back_copy(n).start()

    def take(n):
        block_copy(n).wait_recv()
        back_copy(n).wait_recv()
        mate_copy(HOPS[n][1], half).start()

    for copy in loads[:2]:
        copy.wait()
    turned = tgt_ref[...].T
    for g in range(CHUNKS):
        for r in range(2):
            at = r * FRAME_COLS + g * CHUNK_COLS
            tset[0, g, r * CHUNK_COLS : (r + 1) * CHUNK_COLS] = turned[at : at + CHUNK_COLS]
    back = back_ref[...].astype(jnp.float32)
    bset[0] = jnp.concatenate([back[:, CH * n : CH * n + CH] for n in range(8)], axis=0).astype(jnp.bfloat16)
    for copy in loads[2:]:
        copy.wait()
    picks = dest_ref[...]
    listed = jnp.zeros_like(picks)
    for n in range(4):
        listed = jnp.where((picks >> 10) == n, fetch_ref[0:1, n : n + 1], listed)
    dests = listed * 1024 + (picks & 1023)
    pixel = iota((TILE_ROWS, PIXELS), 1)
    row_of = ((pixel >> 2) & 31) == iota((TILE_ROWS, PIXELS), 0)
    row_hot = jnp.where(row_of, 1.0, 0.0).astype(jnp.bfloat16)
    pixel = iota((TILE_COLS, PIXELS), 1)
    col_of = (pixel >> 7) * 4 + (pixel & 3) == iota((TILE_COLS, PIXELS), 0)
    spread = [
        jnp.dot(part.astype(jnp.float32).astype(jnp.bfloat16), row_hot, preferred_element_type=jnp.float32)
        for part in (dests >> 8, dests & 255)
    ]
    spread = jnp.where(col_of, spread[0] * 256.0 + spread[1], 0.0)
    spread = jnp.sum(spread, axis=0, keepdims=True)
    coarse = jnp.floor(spread * (1.0 / 256.0))
    pair = jnp.concatenate([coarse, spread - coarse * 256.0], axis=0)
    qset[0, PIXELS:] = jnp.concatenate(
        [pair[:, :CH], pair[:, CH:], jnp.zeros((12, CH), jnp.float32)], axis=0
    ).astype(jnp.bfloat16)

    i = iota((PIXELS, PIXELS), 0)
    j = iota((PIXELS, PIXELS), 1)
    wanted = ((i >> 2) & 31) * 8 + (i >> 7) * 4 + (i & 3)
    order = jnp.where(wanted == j, 1.0, 0.0).astype(jnp.bfloat16)
    pixels = project(order, src_ref[...])
    same = ((i >> 5) & 3) == ((j >> 5) & 3)
    attended = attend(
        project(pixels, w_ref[0, 0]), project(pixels, w_ref[0, 1]), project(pixels, w_ref[0, 2]), same
    )
    message = jnp.dot(attended, w_ref[0, 3], preferred_element_type=jnp.float32)
    one = (pixels.astype(jnp.float32) + normed(message, gain_ref[0:1])).astype(jnp.bfloat16)
    halo[0, 16:144] = one[:128]
    halo[1, 16:144] = one[128:]
    pl.semaphore_wait(barrier, 13 + (BLOCKS - 1))
    for copy in halo_copies:
        copy.start()
    for n in (0, 1, 2):
        pass_on(n)
    for copy in halo_copies:
        copy.wait()

    i = iota((128, 320), 0)
    j = iota((128, 320), 1)
    beside = j >= 160
    kk = jnp.where(beside, j - 160, j)
    row, key_row = i >> 2, (kk >> 2) - 4
    low = pb * TILE_ROWS + row < 4
    key_low = ((pb * TILE_ROWS + key_row + FRAME_ROWS) & (FRAME_ROWS - 1)) < 4
    rows_agree = (((row + 4) >> 3) == (kk >> 5)) & (low == key_low)
    for h, edge in ((0, 0), (1, TA - 1)):
        admitted = rows_agree & jnp.logical_not(beside & (ta == edge))
        around = halo[h]
        own = halo[h, 16:144]
        attended = attend(
            project(own, w_ref[1, 0]), project(around, w_ref[1, 1]), project(around, w_ref[1, 2]), admitted
        )
        message = jnp.dot(attended, w_ref[1, 3], preferred_element_type=jnp.float32)
        two = (own.astype(jnp.float32) + normed(message, gain_ref[1:2])).astype(jnp.bfloat16)
        qset[0, h * 128 : (h + 1) * 128] = (two.astype(jnp.float32) * SCORE_LOG2).astype(jnp.bfloat16)

    def nth(k):
        odd = lax.rem(k, 2)
        return lax.rem(odd * lax.div(k + 1, 2) + (1 - odd) * (NZ - lax.div(k, 2)), NZ)

    def query_copy(o):
        held = jnp.where((o == 3), 2, jnp.where((o == 4) | (o == 5), 6, 0))
        return remote(qset.at[held], qset.at[o], q_send.at[o], q_recv.at[o], z_peer(lax.rem(o - held + NZ, NZ)))

    def result_copy(o):
        return remote(res.at[o], rset.at[o], r_send.at[o], r_recv.at[o], z_peer(-o))

    query_copy(1).start()
    query_copy(7).start()
    query_copy(2).start()
    query_copy(6).start()
    take(0)
    pass_on(4)
    take(1)
    pass_on(3)
    pass_on(5)
    take(2)
    pass_on(6)
    for rank in (1, 2, 3):
        mate_copy(rank, other_half).wait_recv()

    sub = iota((8, PIXELS), 0).astype(jnp.float32)
    origins = [(yh + side - 2 * yh * side, lax.rem(x + NX - o, NX)) for side, o in ORIGINS]
    base = (z * 8).astype(jnp.float32)
    row_weights = [(half_of * 64 + column * 2).astype(jnp.float32) for half_of, column in origins]

    def score_chunk(g, late, queries, buffer, top):
        feats = tset[pl.ds(late * GROUP, GROUP), g].reshape(ROW_STEP * CHUNK_COLS, CH)
        scores = lax.dot_general(
            feats, queries, (((1,), (1,)), ((), ())), preferred_element_type=jnp.float32
        )
        buffer[...] = scores
        return jnp.maximum(top, jnp.max(scores.reshape(-1, 8, PIXELS), axis=0))

    def sum_chunk(g, weights, buffer, top, new_top, sums):
        s0, s1, s2 = sums
        fade = jnp.exp2(top - new_top)
        scores = buffer[...].reshape(ROW_STEP, CHUNK_COLS // 8, 8, PIXELS)
        raised = jnp.exp2(scores - new_top[None, None])
        by_row = jnp.sum(raised, axis=1)
        by_col = jnp.sum(raised, axis=0)
        total, col_part = weighted_tree([by_col[n] for n in range(CHUNK_COLS // 8)], (8, 16, 32))
        row_part = tree_sum([by_row[2 * n + 1] for n in range(GROUP)]) + total * base
        for n in range(GROUP):
            row_part = row_part + (by_row[2 * n] + by_row[2 * n + 1]) * weights[n]
        col_part = col_part + total * (sub + float(g * CHUNK_COLS))
        return s0 * fade + row_part, s1 * fade + col_part, s2 * fade + total

    state[0] = jnp.zeros((4, 8, PIXELS), jnp.float32)
    res[0] = jnp.zeros((8, PIXELS), jnp.float32)
    floor = jnp.full((8, PIXELS), NEG, jnp.float32)
    buffers = (even, odd)

    def item(step):
        first, second = step < 5, step < 10
        late = jnp.where(first, 0, jnp.where(second, 1, lax.rem(step, 2)))
        k = jnp.where(first, step, jnp.where(second, step - 5, lax.div(step, 2)))
        return late, nth(k)

    def finish_block(o, late):
        top, s0, s1, s2 = tuple(state[o, m] for m in range(4))
        best = jnp.max(top, axis=0, keepdims=True)
        scale = jnp.exp2(top - best)
        t0 = jnp.sum(s0 * scale, axis=0, keepdims=True)
        t1 = jnp.sum(s1 * scale, axis=0, keepdims=True)
        t2 = jnp.sum(s2 * scale, axis=0, keepdims=True)

        marks = qset[o, PIXELS:].astype(jnp.float32)
        dest = jnp.concatenate(
            [marks[0:1] * 256.0 + marks[1:2], marks[2:3] * 256.0 + marks[3:4]], axis=1
        ).astype(jnp.int32)
        block, off = dest >> 10, dest & 1023
        here = ((block >> 2) & 7) == z
        at = jnp.zeros_like(block)
        for rank, (half_of, column) in enumerate(origins):
            at = jnp.where((block >> 5 == half_of) & ((block & 3) == column), rank * 16, at)
        at = jnp.where(here, at + (off >> 7) * 2, -1000) - late * (GROUP * 16)
        lanes = jnp.where(iota((CH, PIXELS), 0) == (off & 127), 1.0, 0.0).astype(jnp.bfloat16)
        table = bset[pl.ds(late * GROUP, GROUP)].reshape(GROUP * 16, CH)
        picked = jnp.dot(table, lanes, preferred_element_type=jnp.float32)
        line = iota((GROUP * 16, PIXELS), 0)
        back0 = jnp.sum(jnp.where(line == at, picked, 0.0), axis=0, keepdims=True)
        back1 = jnp.sum(jnp.where(line == at + 1, picked, 0.0), axis=0, keepdims=True)
        known = jnp.where(late == 1, res[o, 4:6], 0.0)
        back0, back1 = back0 + known[0:1], back1 + known[1:2]
        pad = jnp.zeros((2, PIXELS), jnp.float32)
        res[o] = jnp.concatenate([best, t0, t1, t2, back0, back1, pad], axis=0)

    def match_step(step, carry):
        late, o = item(step)
        before_late, before_o = item(jnp.maximum(step - 1, 0))
        alone = (step == 0) | (step == 4) | (step == 2 * BLOCKS - 1)
        next_late, next_o = item(jnp.where(alone, step, step + 1))

        @pl.when(step == 1)
        def _():
            query_copy(o).wait_recv()

        @pl.when((next_late == 0) & jnp.logical_not(alone))
        def _():
            query_copy(next_o).wait_recv()

        @pl.when(step == 2)
        def _():
            query_copy(3).start()

        @pl.when(step == 3)
        def _():
            query_copy(5).start()
            query_copy(4).start()

        @pl.when(step == 4)
        def _():
            for hop in (3, 4, 5, 6):
                take(hop)

        @pl.when(step == 5)
        def _():
            for rank in range(GROUP, BLOCKS):
                mate_copy(rank, other_half).wait_recv()

        queries, next_queries = qset[o, :PIXELS], qset[next_o, :PIXELS]

        @pl.when((step == 0) | (step == 1) | (step == 5))
        def _():
            first_top[...] = score_chunk(0, late, queries, even, floor)

        next_top = first_top[...]
        finish_block(before_o, before_late)
        weights = [jnp.where(late == 1, b, a) for a, b in zip(row_weights[:GROUP], row_weights[GROUP:])]
        top = jnp.where(late == 1, state[o, 0], floor)
        sums = tuple(jnp.where(late == 1, state[o, m], 0.0) for m in range(1, 4))
        next_top = jnp.maximum(next_top, top)
        for g in range(CHUNKS):
            last, top = top, next_top
            if g + 1 < CHUNKS:
                next_top = score_chunk(g + 1, late, queries, buffers[(g + 1) % 2], top)
            else:
                next_top = score_chunk(0, next_late, next_queries, even, floor)
            sums = sum_chunk(g, weights, buffers[g % 2], last, top, sums)
        state[o, 0] = top
        for m in range(3):
            state[o, m + 1] = sums[m]

        first_top[...] = next_top

        @pl.when((step > 0) & (before_late == 1) & (before_o > 0))
        def _():
            result_copy(before_o).start()

        return carry

    lax.fori_loop(0, 2 * BLOCKS, match_step, 0)
    finish_block(nth(BLOCKS - 1), 1)
    result_copy(nth(BLOCKS - 1)).start()

    def settle(n, carry):
        remote(res.at[n], rset.at[n], r_send.at[n], r_recv.at[n], mate).wait_recv()
        return carry

    lax.fori_loop(1, BLOCKS, settle, 0)
    parts = [res[0]] + [rset[n] for n in range(1, BLOCKS)]
    best = parts[0]
    for part in parts[1:]:
        best = jnp.maximum(best, part)
    best = best[0:1]
    total = jnp.zeros((8, PIXELS), jnp.float32)
    back = jnp.zeros((8, PIXELS), jnp.float32)
    for part in parts:
        total = total + part * jnp.exp2(part[0:1] - best)
        back = back + part
    p = iota((1, PIXELS), 1)
    row = (pb * TILE_ROWS + ((p >> 2) & 31)).astype(jnp.float32) / FRAME_ROWS
    col = (ta * TILE_COLS + (p >> 7) * 4 + (p & 3)).astype(jnp.float32) / FRAME_COLS
    flow0 = total[1:2] / total[3:4] / FRAME_ROWS - row
    flow1 = total[2:3] / total[3:4] / FRAME_COLS - col
    back0, back1 = back[4:5], back[5:6]
    diff = (flow0 + back0) ** 2 + (flow1 + back1) ** 2
    mag = flow0**2 + flow1**2 + back0**2 + back1**2
    cons = jnp.exp(-diff / (FLOW_ALPHA * mag + FLOW_BETA))
    moved = []
    for value in (flow0, flow1, cons):
        for _ in range(3):
            part = value.astype(jnp.bfloat16).astype(jnp.float32)
            moved.append(jnp.where(col_of, part, 0.0))
            value = value - part
    moved = lax.dot_general(
        jnp.concatenate(moved, axis=0).astype(jnp.bfloat16), row_hot, (((1,), (1,)), ((), ())),
        preferred_element_type=jnp.float32,
    )
    moved = [moved[n * TILE_COLS : (n + 1) * TILE_COLS] for n in range(9)]
    flow_ref[0] = moved[0] + moved[1] + moved[2]
    flow_ref[1] = moved[3] + moved[4] + moved[5]
    cons_ref[...] = moved[6] + moved[7] + moved[8]

    for n in range(NZ - 1):
        block_copy(n).wait_send()
        back_copy(n).wait_send()
        mate_copy(n + 1, half).wait_send()

    def finish(o, carry):
        query_copy(o).wait_send()
        result_copy(o).wait_send()
        return carry

    lax.fori_loop(1, BLOCKS, finish, 0)


def shards(source_feats, target_feats, back_flow, attn_weights, norm_gain, fetch_list, dest_local):
    vmem = pl.BlockSpec(memory_space=pltpu.VMEM)

    def dma(count):
        return pltpu.SemaphoreType.DMA((count,))

    args = (
        source_feats.reshape(PIXELS, CH), target_feats, back_flow, attn_weights, norm_gain, fetch_list, dest_local.T,
    )
    flow, cons = pl.pallas_call(
        kernel,
        out_shape=(
            pltpu.VMEM((2, TILE_COLS, TILE_ROWS), jnp.float32),
            pltpu.VMEM((TILE_COLS, TILE_ROWS), jnp.float32),
        ),
        in_specs=[pl.BlockSpec(memory_space=pl.ANY)] * len(args),
        out_specs=(vmem, vmem),
        scratch_shapes=[pltpu.VMEM(a.shape, a.dtype) for a in args]
        + [dma(len(args))]
        + [
            pltpu.VMEM((NZ, CHUNKS, 2 * CHUNK_COLS, CH), jnp.bfloat16),
            pltpu.VMEM((NZ, 16, CH), jnp.bfloat16),
            pltpu.VMEM((NZ, PIXELS + 16, CH), jnp.bfloat16),
            pltpu.VMEM((2, 320, CH), jnp.bfloat16),
            pltpu.VMEM((BLOCKS, 8, PIXELS), jnp.float32),
            pltpu.VMEM((BLOCKS, 8, PIXELS), jnp.float32),
            pltpu.VMEM((BLOCKS, 4, 8, PIXELS), jnp.float32),
            pltpu.VMEM((8, PIXELS), jnp.float32),
            pltpu.VMEM((ROW_STEP * CHUNK_COLS, PIXELS), jnp.float32),
            pltpu.VMEM((ROW_STEP * CHUNK_COLS, PIXELS), jnp.float32),
        ]
        + [dma(8)] * 12,
        compiler_params=pltpu.CompilerParams(
            collective_id=0, has_side_effects=True, vmem_limit_bytes=60 << 20
        ),
    )(*args)
    return jnp.swapaxes(flow, 1, 2), cons.T


def solution(mesh):
    placed = (
        P("pb", "ta", None),
        P(None, "ta"),
        P(None, "ta"),
        P(),
        P(),
        P(("pb", "ta"), None),
        P("pb", "ta"),
    )
    return jax.shard_map(
        shards,
        mesh=mesh,
        in_specs=placed,
        out_specs=(P(None, "pb", "ta"), P("pb", "ta")),
        check_vma=False,
    )
```

```python
import math

import jax
import jax.numpy as jnp
from jax import lax
from jax.experimental import pallas as pl
from jax.experimental.pallas import tpu as pltpu
from jax.sharding import PartitionSpec as P

MESH = pl.DeviceIdType.MESH
NORM_EPSILON = 1e-05
MATCH_GAIN = 2.0
FLOW_ALPHA = 0.01
FLOW_BETA = 0.5
CH = 128
PB, TA = 4, 64
NX, NZ = 4, 8
FRAME_ROWS, FRAME_COLS = 128, 512
TILE_ROWS, TILE_COLS = 32, 8
PIXELS = TILE_ROWS * TILE_COLS
BLOCKS = NZ
LAST = 2 * BLOCKS - 1
GROUP = 4
ROW_STEP = 2 * GROUP
ORIGINS = ((0, 0), (0, 1), (0, 3), (1, 0), (0, 2), (1, 1), (1, 3), (1, 2))
HOPS = ((0, 1, 0, 1), (0, 2, 0, -1), (0, 3, 1, 0), (2, 4, 0, -1), (1, 5, 1, 0), (2, 6, 1, 0), (3, 7, 0, 2))
CHUNKS, CHUNK_COLS = 8, 64
NEG = -1e30
SCORE_LOG2 = MATCH_GAIN / math.sqrt(CH) * math.log2(math.e)


def tree_sum(xs):
    xs = list(xs)
    while len(xs) > 1:
        xs = [xs[i] + xs[i + 1] for i in range(0, len(xs), 2)]
    return xs[0]


def weighted_tree(xs, weights):
    odd, cur = [], list(xs)
    while len(cur) > 1:
        odd.append(tree_sum(cur[1::2]))
        cur = [cur[i] + cur[i + 1] for i in range(0, len(cur), 2)]
    total = None
    for value, weight in zip(odd, weights):
        term = value * float(weight)
        total = term if total is None else total + term
    return cur[0], total


def normed(message, gain):
    center = message - jnp.mean(message, axis=-1, keepdims=True)
    spread = jnp.mean(center * center, axis=-1, keepdims=True)
    return center * lax.rsqrt(spread + NORM_EPSILON) * gain


def attend(queries, keys, values, admitted):
    scores = lax.dot_general(
        queries, keys, (((1,), (1,)), ((), ())), preferred_element_type=jnp.float32
    ) * (1.0 / math.sqrt(CH))
    scores = jnp.where(admitted, scores, NEG)
    raised = jnp.exp(scores - jnp.max(scores, axis=-1, keepdims=True))
    weights = (raised / jnp.sum(raised, axis=-1, keepdims=True)).astype(jnp.bfloat16)
    return jnp.dot(weights, values, preferred_element_type=jnp.float32).astype(jnp.bfloat16)


def project(pixels, matrix):
    return jnp.dot(pixels, matrix, preferred_element_type=jnp.float32).astype(jnp.bfloat16)


def iota(shape, axis):
    return lax.broadcasted_iota(jnp.int32, shape, axis)


def place():
    pb, ta = lax.axis_index("pb"), lax.axis_index("ta")
    yh, z, x = lax.div(ta, 32), lax.rem(lax.div(ta, NX), NZ), lax.rem(ta, NX)
    return pb, ta, yh, z, x


def kernel(
    src_hbm, tgt_hbm, back_hbm, w_hbm, gain_hbm, fetch_hbm, dest_hbm, flow_ref, cons_ref,
    src_ref, tgt_ref, back_ref, w_ref, gain_ref, fetch_ref, dest_ref, load_sem,
    tset, bset, qset, halo, res, rset, state, first_top, even, odd,
    t_send, t_recv, f_send, f_recv, b_send, b_recv,
    q_send, q_recv, r_send, r_recv, h_send, h_recv,
):
    pb, ta, yh, z, x = place()
    core = lax.rem(pb, 2)
    mate = (pb + 1 - 2 * core, ta)
    up, down = lax.rem(pb + PB - 1, PB), lax.rem(pb + 1, PB)
    left, right = lax.rem(ta + TA - 1, TA), lax.rem(ta + 1, TA)

    def z_peer(offset):
        return (pb, yh * 32 + lax.rem(z + offset + NZ, NZ) * NX + x)

    def x_peer(side, offset):
        far = core + 2 * (1 - lax.div(pb, 2))
        half = yh + side - 2 * yh * side
        return (pb + side * (far - pb), half * 32 + z * NX + lax.rem(x + offset + NX, NX))

    def remote(src, dst, send, recv, device):
        return pltpu.make_async_remote_copy(
            src_ref=src, dst_ref=dst, send_sem=send, recv_sem=recv, device_id=device, device_id_type=MESH
        )

    halo_copies = [
        remote(halo.at[:, 16:32], halo.at[:, 144:160], h_send.at[0], h_recv.at[0], (up, ta)),
        remote(halo.at[:, 128:144], halo.at[:, 0:16], h_send.at[1], h_recv.at[1], (down, ta)),
        remote(halo.at[1, 16:144], halo.at[0, 176:304], h_send.at[2], h_recv.at[2], (pb, right)),
        remote(halo.at[0, 16:144], halo.at[1, 176:304], h_send.at[3], h_recv.at[3], (pb, left)),
        remote(halo.at[1, 16:32], halo.at[0, 304:320], h_send.at[4], h_recv.at[4], (up, right)),
        remote(halo.at[1, 128:144], halo.at[0, 160:176], h_send.at[5], h_recv.at[5], (down, right)),
        remote(halo.at[0, 16:32], halo.at[1, 304:320], h_send.at[6], h_recv.at[6], (up, left)),
        remote(halo.at[0, 128:144], halo.at[1, 160:176], h_send.at[7], h_recv.at[7], (down, left)),
    ]

    loads = [
        pltpu.make_async_copy(a, b, load_sem.at[n])
        for n, (a, b) in enumerate(
            (
                (tgt_hbm, tgt_ref), (back_hbm, back_ref), (src_hbm, src_ref), (w_hbm, w_ref),
                (gain_hbm, gain_ref), (fetch_hbm, fetch_ref), (dest_hbm, dest_ref),
            )
        )
    ]
    for copy in loads:
        copy.start()

    barrier = pltpu.get_barrier_semaphore()
    for device in (
        (up, ta), (down, ta), (pb, right), (pb, left), (up, right), (down, right), (up, left), (down, left), mate,
        x_peer(0, 1), x_peer(0, 2), x_peer(0, 3), x_peer(1, 0),
    ):
        pl.semaphore_signal(barrier, inc=1, device_id=device, device_id_type=MESH)

    def greet(o, carry):
        pl.semaphore_signal(barrier, inc=1, device_id=z_peer(o), device_id_type=MESH)
        return carry

    lax.fori_loop(1, NZ, greet, 0)

    half = pl.ds(core * (CHUNKS // 2), CHUNKS // 2)
    other_half = pl.ds((1 - core) * (CHUNKS // 2), CHUNKS // 2)

    def block_copy(n):
        held, rank, side, steps = HOPS[n]
        return remote(tset.at[held, half], tset.at[rank, half], t_send.at[n], t_recv.at[rank], x_peer(side, steps))

    def back_copy(n):
        held, rank, side, steps = HOPS[n]
        return remote(bset.at[held], bset.at[rank], b_send.at[n], b_recv.at[rank], x_peer(side, steps))

    def mate_copy(rank, part):
        return remote(tset.at[rank, part], tset.at[rank, part], f_send.at[rank], f_recv.at[rank], mate)

    def pass_on(n):
        block_copy(n).start()
        back_copy(n).start()

    def take(n):
        block_copy(n).wait_recv()
        back_copy(n).wait_recv()
        mate_copy(HOPS[n][1], half).start()

    for copy in loads[:2]:
        copy.wait()
    turned = tgt_ref[...].T
    for g in range(CHUNKS):
        for r in range(2):
            at = r * FRAME_COLS + g * CHUNK_COLS
            tset[0, g, r * CHUNK_COLS : (r + 1) * CHUNK_COLS] = turned[at : at + CHUNK_COLS]
    back = back_ref[...].astype(jnp.float32)
    bset[0] = jnp.concatenate([back[:, CH * n : CH * n + CH] for n in range(8)], axis=0).astype(jnp.bfloat16)
    for copy in loads[2:]:
        copy.wait()
    picks = dest_ref[...]
    listed = jnp.zeros_like(picks)
    for n in range(4):
        listed = jnp.where((picks >> 10) == n, fetch_ref[0:1, n : n + 1], listed)
    dests = listed * 1024 + (picks & 1023)
    pixel = iota((TILE_ROWS, PIXELS), 1)
    row_of = ((pixel >> 2) & 31) == iota((TILE_ROWS, PIXELS), 0)
    row_hot = jnp.where(row_of, 1.0, 0.0).astype(jnp.bfloat16)
    pixel = iota((TILE_COLS, PIXELS), 1)
    col_of = (pixel >> 7) * 4 + (pixel & 3) == iota((TILE_COLS, PIXELS), 0)
    spread = [
        jnp.dot(part.astype(jnp.float32).astype(jnp.bfloat16), row_hot, preferred_element_type=jnp.float32)
        for part in (dests >> 8, dests & 255)
    ]
    spread = jnp.where(col_of, spread[0] * 256.0 + spread[1], 0.0)
    spread = jnp.sum(spread, axis=0, keepdims=True)
    coarse = jnp.floor(spread * (1.0 / 256.0))
    pair = jnp.concatenate([coarse, spread - coarse * 256.0], axis=0)
    qset[0, PIXELS:] = jnp.concatenate(
        [pair[:, :CH], pair[:, CH:], jnp.zeros((12, CH), jnp.float32)], axis=0
    ).astype(jnp.bfloat16)

    i = iota((PIXELS, PIXELS), 0)
    j = iota((PIXELS, PIXELS), 1)
    wanted = ((i >> 2) & 31) * 8 + (i >> 7) * 4 + (i & 3)
    order = jnp.where(wanted == j, 1.0, 0.0).astype(jnp.bfloat16)
    pixels = project(order, src_ref[...])
    same = ((i >> 5) & 3) == ((j >> 5) & 3)
    attended = attend(
        project(pixels, w_ref[0, 0]), project(pixels, w_ref[0, 1]), project(pixels, w_ref[0, 2]), same
    )
    message = jnp.dot(attended, w_ref[0, 3], preferred_element_type=jnp.float32)
    one = (pixels.astype(jnp.float32) + normed(message, gain_ref[0:1])).astype(jnp.bfloat16)
    halo[0, 16:144] = one[:128]
    halo[1, 16:144] = one[128:]
    pl.semaphore_wait(barrier, 13 + (BLOCKS - 1))
    for copy in halo_copies:
        copy.start()
    for n in (0, 1, 2):
        pass_on(n)
    for copy in halo_copies:
        copy.wait()

    i = iota((128, 320), 0)
    j = iota((128, 320), 1)
    beside = j >= 160
    kk = jnp.where(beside, j - 160, j)
    row, key_row = i >> 2, (kk >> 2) - 4
    low = pb * TILE_ROWS + row < 4
    key_low = ((pb * TILE_ROWS + key_row + FRAME_ROWS) & (FRAME_ROWS - 1)) < 4
    rows_agree = (((row + 4) >> 3) == (kk >> 5)) & (low == key_low)
    for h, edge in ((0, 0), (1, TA - 1)):
        admitted = rows_agree & jnp.logical_not(beside & (ta == edge))
        around = halo[h]
        own = halo[h, 16:144]
        attended = attend(
            project(own, w_ref[1, 0]), project(around, w_ref[1, 1]), project(around, w_ref[1, 2]), admitted
        )
        message = jnp.dot(attended, w_ref[1, 3], preferred_element_type=jnp.float32)
        two = (own.astype(jnp.float32) + normed(message, gain_ref[1:2])).astype(jnp.bfloat16)
        qset[0, h * 128 : (h + 1) * 128] = (two.astype(jnp.float32) * SCORE_LOG2).astype(jnp.bfloat16)

    def nth(k):
        odd = lax.rem(k, 2)
        return lax.rem(odd * lax.div(k + 1, 2) + (1 - odd) * (NZ - lax.div(k, 2)), NZ)

    def query_copy(o):
        held = jnp.where((o == 3), 2, jnp.where((o == 4) | (o == 5), 6, 0))
        return remote(qset.at[held], qset.at[o], q_send.at[o], q_recv.at[o], z_peer(lax.rem(o - held + NZ, NZ)))

    def result_copy(o):
        return remote(res.at[o], rset.at[o], r_send.at[o], r_recv.at[o], z_peer(-o))

    query_copy(1).start()
    query_copy(7).start()
    query_copy(2).start()
    query_copy(6).start()
    take(0)
    pass_on(4)
    take(1)
    pass_on(3)
    pass_on(5)
    take(2)
    pass_on(6)
    for rank in (1, 2, 3):
        mate_copy(rank, other_half).wait_recv()

    sub = iota((8, PIXELS), 0).astype(jnp.float32)
    origins = [(yh + side - 2 * yh * side, lax.rem(x + NX - o, NX)) for side, o in ORIGINS]
    base = (z * 8).astype(jnp.float32)
    row_weights = [(half_of * 64 + column * 2).astype(jnp.float32) for half_of, column in origins]

    def score_chunk(g, late, queries, buffer, top):
        feats = tset[pl.ds(late * GROUP, GROUP), g].reshape(ROW_STEP * CHUNK_COLS, CH)
        scores = lax.dot_general(
            feats, queries, (((1,), (1,)), ((), ())), preferred_element_type=jnp.float32
        )
        buffer[...] = scores
        return jnp.maximum(top, jnp.max(scores.reshape(-1, 8, PIXELS), axis=0))

    def sum_chunk(g, weights, buffer, top, new_top, sums):
        s0, s1, s2 = sums
        fade = jnp.exp2(top - new_top)
        scores = buffer[...].reshape(ROW_STEP, CHUNK_COLS // 8, 8, PIXELS)
        raised = jnp.exp2(scores - new_top[None, None])
        by_row = jnp.sum(raised, axis=1)
        by_col = jnp.sum(raised, axis=0)
        total, col_part = weighted_tree([by_col[n] for n in range(CHUNK_COLS // 8)], (8, 16, 32))
        row_part = tree_sum([by_row[2 * n + 1] for n in range(GROUP)]) + total * base
        for n in range(GROUP):
            row_part = row_part + (by_row[2 * n] + by_row[2 * n + 1]) * weights[n]
        col_part = col_part + total * (sub + float(g * CHUNK_COLS))
        return s0 * fade + row_part, s1 * fade + col_part, s2 * fade + total

    state[0] = jnp.zeros((4, 8, PIXELS), jnp.float32)
    res[0] = jnp.zeros((8, PIXELS), jnp.float32)
    floor = jnp.full((8, PIXELS), NEG, jnp.float32)
    buffers = (even, odd)

    def item(step):
        first, second, last = step < 5, step < 9, step == LAST
        late = jnp.where(first, 0, jnp.where(second | last, 1, lax.rem(step + 1, 2)))
        k = jnp.where(first, step, jnp.where(second, step - 4, jnp.where(last, 0, lax.div(step + 1, 2))))
        return late, nth(k)

    def finish_block(o, late):
        top, s0, s1, s2 = tuple(state[o, m] for m in range(4))
        best = jnp.max(top, axis=0, keepdims=True)
        scale = jnp.exp2(top - best)
        t0 = jnp.sum(s0 * scale, axis=0, keepdims=True)
        t1 = jnp.sum(s1 * scale, axis=0, keepdims=True)
        t2 = jnp.sum(s2 * scale, axis=0, keepdims=True)

        marks = qset[o, PIXELS:].astype(jnp.float32)
        dest = jnp.concatenate(
            [marks[0:1] * 256.0 + marks[1:2], marks[2:3] * 256.0 + marks[3:4]], axis=1
        ).astype(jnp.int32)
        block, off = dest >> 10, dest & 1023
        here = ((block >> 2) & 7) == z
        at = jnp.zeros_like(block)
        for rank, (half_of, column) in enumerate(origins):
            at = jnp.where((block >> 5 == half_of) & ((block & 3) == column), rank * 16, at)
        at = jnp.where(here, at + (off >> 7) * 2, -1000) - late * (GROUP * 16)
        lanes = jnp.where(iota((CH, PIXELS), 0) == (off & 127), 1.0, 0.0).astype(jnp.bfloat16)
        table = bset[pl.ds(late * GROUP, GROUP)].reshape(GROUP * 16, CH)
        picked = jnp.dot(table, lanes, preferred_element_type=jnp.float32)
        line = iota((GROUP * 16, PIXELS), 0)
        back0 = jnp.sum(jnp.where(line == at, picked, 0.0), axis=0, keepdims=True)
        back1 = jnp.sum(jnp.where(line == at + 1, picked, 0.0), axis=0, keepdims=True)
        known = jnp.where(late == 1, res[o, 4:6], 0.0)
        back0, back1 = back0 + known[0:1], back1 + known[1:2]
        pad = jnp.zeros((2, PIXELS), jnp.float32)
        res[o] = jnp.concatenate([best, t0, t1, t2, back0, back1, pad], axis=0)

    def match_step(step, carry):
        late, o = item(step)
        before_late, before_o = item(jnp.where(step == LAST, 0, jnp.maximum(step - 1, 0)))
        alone = (step == 0) | (step == 4) | (step == LAST)
        next_late, next_o = item(jnp.where(alone, step, step + 1))

        @pl.when(step == 1)
        def _():
            query_copy(o).wait_recv()

        @pl.when((next_late == 0) & jnp.logical_not(alone))
        def _():
            query_copy(next_o).wait_recv()

        @pl.when(step == 2)
        def _():
            query_copy(3).start()

        @pl.when(step == 3)
        def _():
            query_copy(5).start()
            query_copy(4).start()

        @pl.when(step == 4)
        def _():
            for hop in (3, 4, 5, 6):
                take(hop)

        @pl.when(step == 5)
        def _():
            for rank in range(GROUP, BLOCKS):
                mate_copy(rank, other_half).wait_recv()

        queries, next_queries = qset[o, :PIXELS], qset[next_o, :PIXELS]

        @pl.when((step == 0) | (step == 1) | (step == 5))
        def _():
            first_top[...] = score_chunk(0, late, queries, even, floor)

        @pl.when(step == LAST)
        def _():
            done_late, done_o = item(LAST - 1)
            finish_block(done_o, done_late)
            result_copy(done_o).start()

        next_top = first_top[...]
        finish_block(before_o, before_late)
        weights = [jnp.where(late == 1, b, a) for a, b in zip(row_weights[:GROUP], row_weights[GROUP:])]
        top = jnp.where(late == 1, state[o, 0], floor)
        sums = tuple(jnp.where(late == 1, state[o, m], 0.0) for m in range(1, 4))
        next_top = jnp.maximum(next_top, top)
        for g in range(CHUNKS):
            last, top = top, next_top
            if g + 1 < CHUNKS:
                next_top = score_chunk(g + 1, late, queries, buffers[(g + 1) % 2], top)
            else:
                next_top = score_chunk(0, next_late, next_queries, even, floor)
            sums = sum_chunk(g, weights, buffers[g % 2], last, top, sums)
        state[o, 0] = top
        for m in range(3):
            state[o, m + 1] = sums[m]

        first_top[...] = next_top

        @pl.when((step > 0) & (before_late == 1) & (before_o > 0))
        def _():
            result_copy(before_o).start()

        return carry

    lax.fori_loop(0, 2 * BLOCKS, match_step, 0)
    finish_block(0, 1)

    def settle(n, carry):
        remote(res.at[n], rset.at[n], r_send.at[n], r_recv.at[n], mate).wait_recv()
        return carry

    lax.fori_loop(1, BLOCKS, settle, 0)
    parts = [res[0]] + [rset[n] for n in range(1, BLOCKS)]
    best = parts[0]
    for part in parts[1:]:
        best = jnp.maximum(best, part)
    best = best[0:1]
    total = jnp.zeros((8, PIXELS), jnp.float32)
    back = jnp.zeros((8, PIXELS), jnp.float32)
    for part in parts:
        total = total + part * jnp.exp2(part[0:1] - best)
        back = back + part
    p = iota((1, PIXELS), 1)
    row = (pb * TILE_ROWS + ((p >> 2) & 31)).astype(jnp.float32) / FRAME_ROWS
    col = (ta * TILE_COLS + (p >> 7) * 4 + (p & 3)).astype(jnp.float32) / FRAME_COLS
    flow0 = total[1:2] / total[3:4] / FRAME_ROWS - row
    flow1 = total[2:3] / total[3:4] / FRAME_COLS - col
    back0, back1 = back[4:5], back[5:6]
    diff = (flow0 + back0) ** 2 + (flow1 + back1) ** 2
    mag = flow0**2 + flow1**2 + back0**2 + back1**2
    cons = jnp.exp(-diff / (FLOW_ALPHA * mag + FLOW_BETA))
    moved = []
    for value in (flow0, flow1, cons):
        for _ in range(3):
            part = value.astype(jnp.bfloat16).astype(jnp.float32)
            moved.append(jnp.where(col_of, part, 0.0))
            value = value - part
    moved = lax.dot_general(
        jnp.concatenate(moved, axis=0).astype(jnp.bfloat16), row_hot, (((1,), (1,)), ((), ())),
        preferred_element_type=jnp.float32,
    )
    moved = [moved[n * TILE_COLS : (n + 1) * TILE_COLS] for n in range(9)]
    flow_ref[0] = moved[0] + moved[1] + moved[2]
    flow_ref[1] = moved[3] + moved[4] + moved[5]
    cons_ref[...] = moved[6] + moved[7] + moved[8]

    for n in range(NZ - 1):
        block_copy(n).wait_send()
        back_copy(n).wait_send()
        mate_copy(n + 1, half).wait_send()

    def finish(o, carry):
        query_copy(o).wait_send()
        result_copy(o).wait_send()
        return carry

    lax.fori_loop(1, BLOCKS, finish, 0)


def shards(source_feats, target_feats, back_flow, attn_weights, norm_gain, fetch_list, dest_local):
    vmem = pl.BlockSpec(memory_space=pltpu.VMEM)

    def dma(count):
        return pltpu.SemaphoreType.DMA((count,))

    args = (
        source_feats.reshape(PIXELS, CH), target_feats, back_flow, attn_weights, norm_gain, fetch_list, dest_local.T,
    )
    flow, cons = pl.pallas_call(
        kernel,
        out_shape=(
            pltpu.VMEM((2, TILE_COLS, TILE_ROWS), jnp.float32),
            pltpu.VMEM((TILE_COLS, TILE_ROWS), jnp.float32),
        ),
        in_specs=[pl.BlockSpec(memory_space=pl.ANY)] * len(args),
        out_specs=(vmem, vmem),
        scratch_shapes=[pltpu.VMEM(a.shape, a.dtype) for a in args]
        + [dma(len(args))]
        + [
            pltpu.VMEM((NZ, CHUNKS, 2 * CHUNK_COLS, CH), jnp.bfloat16),
            pltpu.VMEM((NZ, 16, CH), jnp.bfloat16),
            pltpu.VMEM((NZ, PIXELS + 16, CH), jnp.bfloat16),
            pltpu.VMEM((2, 320, CH), jnp.bfloat16),
            pltpu.VMEM((BLOCKS, 8, PIXELS), jnp.float32),
            pltpu.VMEM((BLOCKS, 8, PIXELS), jnp.float32),
            pltpu.VMEM((BLOCKS, 4, 8, PIXELS), jnp.float32),
            pltpu.VMEM((8, PIXELS), jnp.float32),
            pltpu.VMEM((ROW_STEP * CHUNK_COLS, PIXELS), jnp.float32),
            pltpu.VMEM((ROW_STEP * CHUNK_COLS, PIXELS), jnp.float32),
        ]
        + [dma(8)] * 12,
        compiler_params=pltpu.CompilerParams(
            collective_id=0, has_side_effects=True, vmem_limit_bytes=60 << 20
        ),
    )(*args)
    return jnp.swapaxes(flow, 1, 2), cons.T


def solution(mesh):
    placed = (
        P("pb", "ta", None),
        P(None, "ta"),
        P(None, "ta"),
        P(),
        P(),
        P(("pb", "ta"), None),
        P("pb", "ta"),
    )
    return jax.shard_map(
        shards,
        mesh=mesh,
        in_specs=placed,
        out_specs=(P(None, "pb", "ta"), P("pb", "ta")),
        check_vma=False,
    )
```

```python
import math

import jax
import jax.numpy as jnp
from jax import lax
from jax.experimental import pallas as pl
from jax.experimental.pallas import tpu as pltpu
from jax.sharding import PartitionSpec as P

MESH = pl.DeviceIdType.MESH
NORM_EPSILON = 1e-05
MATCH_GAIN = 2.0
FLOW_ALPHA = 0.01
FLOW_BETA = 0.5
CH = 128
PB, TA = 4, 64
NX, NZ = 4, 8
FRAME_ROWS, FRAME_COLS = 128, 512
TILE_ROWS, TILE_COLS = 32, 8
PIXELS = TILE_ROWS * TILE_COLS
BLOCKS = NZ
LAST = 2 * BLOCKS - 1
GROUP = 4
ROW_STEP = 2 * GROUP
ORIGINS = ((0, 0), (0, 1), (0, 3), (1, 0), (0, 2), (1, 1), (1, 3), (1, 2))
HOPS = ((0, 1, 0, 1), (0, 2, 0, -1), (0, 3, 1, 0), (2, 4, 0, -1), (1, 5, 1, 0), (2, 6, 1, 0), (3, 7, 0, 2))
CHUNKS, CHUNK_COLS = 8, 64
NEG = -1e30
SCORE_LOG2 = MATCH_GAIN / math.sqrt(CH) * math.log2(math.e)


def tree_sum(xs):
    xs = list(xs)
    while len(xs) > 1:
        xs = [xs[i] + xs[i + 1] for i in range(0, len(xs), 2)]
    return xs[0]


def weighted_tree(xs, weights):
    odd, cur = [], list(xs)
    while len(cur) > 1:
        odd.append(tree_sum(cur[1::2]))
        cur = [cur[i] + cur[i + 1] for i in range(0, len(cur), 2)]
    total = None
    for value, weight in zip(odd, weights):
        term = value * float(weight)
        total = term if total is None else total + term
    return cur[0], total


def normed(message, gain):
    center = message - jnp.mean(message, axis=-1, keepdims=True)
    spread = jnp.mean(center * center, axis=-1, keepdims=True)
    return center * lax.rsqrt(spread + NORM_EPSILON) * gain


def attend(queries, keys, values, admitted):
    scores = lax.dot_general(
        queries, keys, (((1,), (1,)), ((), ())), preferred_element_type=jnp.float32
    ) * (1.0 / math.sqrt(CH))
    scores = jnp.where(admitted, scores, NEG)
    raised = jnp.exp(scores - jnp.max(scores, axis=-1, keepdims=True))
    weights = (raised / jnp.sum(raised, axis=-1, keepdims=True)).astype(jnp.bfloat16)
    return jnp.dot(weights, values, preferred_element_type=jnp.float32).astype(jnp.bfloat16)


def project(pixels, matrix):
    return jnp.dot(pixels, matrix, preferred_element_type=jnp.float32).astype(jnp.bfloat16)


def iota(shape, axis):
    return lax.broadcasted_iota(jnp.int32, shape, axis)


def place():
    pb, ta = lax.axis_index("pb"), lax.axis_index("ta")
    yh, z, x = lax.div(ta, 32), lax.rem(lax.div(ta, NX), NZ), lax.rem(ta, NX)
    return pb, ta, yh, z, x


def kernel(
    src_hbm, tgt_hbm, back_hbm, w_hbm, gain_hbm, fetch_hbm, dest_hbm, flow_ref, cons_ref,
    src_ref, tgt_ref, back_ref, w_ref, gain_ref, fetch_ref, dest_ref, load_sem,
    tset, bset, qset, halo, res, rset, state, first_top, even, odd,
    t_send, t_recv, f_send, f_recv, b_send, b_recv,
    q_send, q_recv, r_send, r_recv, h_send, h_recv,
):
    pb, ta, yh, z, x = place()
    core = lax.rem(pb, 2)
    mate = (pb + 1 - 2 * core, ta)
    up, down = lax.rem(pb + PB - 1, PB), lax.rem(pb + 1, PB)
    left, right = lax.rem(ta + TA - 1, TA), lax.rem(ta + 1, TA)

    def z_peer(offset):
        return (pb, yh * 32 + lax.rem(z + offset + NZ, NZ) * NX + x)

    def x_peer(side, offset):
        far = core + 2 * (1 - lax.div(pb, 2))
        half = yh + side - 2 * yh * side
        return (pb + side * (far - pb), half * 32 + z * NX + lax.rem(x + offset + NX, NX))

    def remote(src, dst, send, recv, device):
        return pltpu.make_async_remote_copy(
            src_ref=src, dst_ref=dst, send_sem=send, recv_sem=recv, device_id=device, device_id_type=MESH
        )

    halo_copies = [
        remote(halo.at[:, 16:32], halo.at[:, 144:160], h_send.at[0], h_recv.at[0], (up, ta)),
        remote(halo.at[:, 128:144], halo.at[:, 0:16], h_send.at[1], h_recv.at[1], (down, ta)),
        remote(halo.at[1, 16:144], halo.at[0, 176:304], h_send.at[2], h_recv.at[2], (pb, right)),
        remote(halo.at[0, 16:144], halo.at[1, 176:304], h_send.at[3], h_recv.at[3], (pb, left)),
        remote(halo.at[1, 16:32], halo.at[0, 304:320], h_send.at[4], h_recv.at[4], (up, right)),
        remote(halo.at[1, 128:144], halo.at[0, 160:176], h_send.at[5], h_recv.at[5], (down, right)),
        remote(halo.at[0, 16:32], halo.at[1, 304:320], h_send.at[6], h_recv.at[6], (up, left)),
        remote(halo.at[0, 128:144], halo.at[1, 160:176], h_send.at[7], h_recv.at[7], (down, left)),
    ]

    loads = [
        pltpu.make_async_copy(a, b, load_sem.at[n])
        for n, (a, b) in enumerate(
            (
                (tgt_hbm, tgt_ref), (back_hbm, back_ref), (src_hbm, src_ref), (w_hbm, w_ref),
                (gain_hbm, gain_ref), (fetch_hbm, fetch_ref), (dest_hbm, dest_ref),
            )
        )
    ]
    for copy in loads:
        copy.start()

    barrier = pltpu.get_barrier_semaphore()
    for device in (
        (up, ta), (down, ta), (pb, right), (pb, left), (up, right), (down, right), (up, left), (down, left), mate,
        x_peer(0, 1), x_peer(0, 2), x_peer(0, 3), x_peer(1, 0),
    ):
        pl.semaphore_signal(barrier, inc=1, device_id=device, device_id_type=MESH)

    def greet(o, carry):
        pl.semaphore_signal(barrier, inc=1, device_id=z_peer(o), device_id_type=MESH)
        return carry

    lax.fori_loop(1, NZ, greet, 0)

    half = pl.ds(core * (CHUNKS // 2), CHUNKS // 2)
    other_half = pl.ds((1 - core) * (CHUNKS // 2), CHUNKS // 2)

    def block_copy(n):
        held, rank, side, steps = HOPS[n]
        return remote(tset.at[held, half], tset.at[rank, half], t_send.at[n], t_recv.at[rank], x_peer(side, steps))

    def back_copy(n):
        held, rank, side, steps = HOPS[n]
        return remote(bset.at[held], bset.at[rank], b_send.at[n], b_recv.at[rank], x_peer(side, steps))

    def mate_copy(rank, part):
        return remote(tset.at[rank, part], tset.at[rank, part], f_send.at[rank], f_recv.at[rank], mate)

    def pass_on(n):
        block_copy(n).start()
        back_copy(n).start()

    def take(n):
        block_copy(n).wait_recv()
        back_copy(n).wait_recv()
        mate_copy(HOPS[n][1], half).start()

    for copy in loads[:2]:
        copy.wait()
    turned = tgt_ref[...].T
    for g in range(CHUNKS):
        for r in range(2):
            at = r * FRAME_COLS + g * CHUNK_COLS
            tset[0, g, r * CHUNK_COLS : (r + 1) * CHUNK_COLS] = turned[at : at + CHUNK_COLS]
    back = back_ref[...].astype(jnp.float32)
    bset[0] = jnp.concatenate([back[:, CH * n : CH * n + CH] for n in range(8)], axis=0).astype(jnp.bfloat16)
    for copy in loads[2:]:
        copy.wait()
    picks = dest_ref[...]
    listed = jnp.zeros_like(picks)
    for n in range(4):
        listed = jnp.where((picks >> 10) == n, fetch_ref[0:1, n : n + 1], listed)
    dests = listed * 1024 + (picks & 1023)
    pixel = iota((TILE_ROWS, PIXELS), 1)
    row_of = ((pixel >> 2) & 31) == iota((TILE_ROWS, PIXELS), 0)
    row_hot = jnp.where(row_of, 1.0, 0.0).astype(jnp.bfloat16)
    pixel = iota((TILE_COLS, PIXELS), 1)
    col_of = (pixel >> 7) * 4 + (pixel & 3) == iota((TILE_COLS, PIXELS), 0)
    spread = [
        jnp.dot(part.astype(jnp.float32).astype(jnp.bfloat16), row_hot, preferred_element_type=jnp.float32)
        for part in (dests >> 8, dests & 255)
    ]
    spread = jnp.where(col_of, spread[0] * 256.0 + spread[1], 0.0)
    spread = jnp.sum(spread, axis=0, keepdims=True)
    coarse = jnp.floor(spread * (1.0 / 256.0))
    pair = jnp.concatenate([coarse, spread - coarse * 256.0], axis=0)
    qset[0, PIXELS:] = jnp.concatenate(
        [pair[:, :CH], pair[:, CH:], jnp.zeros((12, CH), jnp.float32)], axis=0
    ).astype(jnp.bfloat16)

    i = iota((PIXELS, PIXELS), 0)
    j = iota((PIXELS, PIXELS), 1)
    wanted = ((i >> 2) & 31) * 8 + (i >> 7) * 4 + (i & 3)
    order = jnp.where(wanted == j, 1.0, 0.0).astype(jnp.bfloat16)
    pixels = project(order, src_ref[...])
    same = ((i >> 5) & 3) == ((j >> 5) & 3)
    attended = attend(
        project(pixels, w_ref[0, 0]), project(pixels, w_ref[0, 1]), project(pixels, w_ref[0, 2]), same
    )
    message = jnp.dot(attended, w_ref[0, 3], preferred_element_type=jnp.float32)
    one = (pixels.astype(jnp.float32) + normed(message, gain_ref[0:1])).astype(jnp.bfloat16)
    halo[0, 16:144] = one[:128]
    halo[1, 16:144] = one[128:]
    pl.semaphore_wait(barrier, 13 + (BLOCKS - 1))
    for copy in halo_copies:
        copy.start()
    for n in (0, 1, 2):
        pass_on(n)

    i = iota((128, 320), 0)
    j = iota((128, 320), 1)
    beside = j >= 160
    kk = jnp.where(beside, j - 160, j)
    row, key_row = i >> 2, (kk >> 2) - 4
    low = pb * TILE_ROWS + row < 4
    key_low = ((pb * TILE_ROWS + key_row + FRAME_ROWS) & (FRAME_ROWS - 1)) < 4
    rows_agree = (((row + 4) >> 3) == (kk >> 5)) & (low == key_low)
    admitted = [rows_agree & jnp.logical_not(beside & (ta == edge)) for edge in (0, TA - 1)]
    own_queries = [project(one[h * 128 : (h + 1) * 128], w_ref[1, 0]) for h in range(2)]
    for copy in halo_copies:
        copy.wait()
    for h in range(2):
        around = halo[h]
        own = halo[h, 16:144]
        attended = attend(
            own_queries[h], project(around, w_ref[1, 1]), project(around, w_ref[1, 2]), admitted[h]
        )
        message = jnp.dot(attended, w_ref[1, 3], preferred_element_type=jnp.float32)
        two = (own.astype(jnp.float32) + normed(message, gain_ref[1:2])).astype(jnp.bfloat16)
        qset[0, h * 128 : (h + 1) * 128] = (two.astype(jnp.float32) * SCORE_LOG2).astype(jnp.bfloat16)

    def nth(k):
        odd = lax.rem(k, 2)
        return lax.rem(odd * lax.div(k + 1, 2) + (1 - odd) * (NZ - lax.div(k, 2)), NZ)

    def query_copy(o):
        held = jnp.where((o == 3), 2, jnp.where((o == 4) | (o == 5), 6, 0))
        return remote(qset.at[held], qset.at[o], q_send.at[o], q_recv.at[o], z_peer(lax.rem(o - held + NZ, NZ)))

    def result_copy(o):
        return remote(res.at[o], rset.at[o], r_send.at[o], r_recv.at[o], z_peer(-o))

    query_copy(1).start()
    query_copy(7).start()
    query_copy(2).start()
    query_copy(6).start()
    take(0)
    pass_on(4)
    take(1)
    pass_on(3)
    pass_on(5)
    take(2)
    pass_on(6)
    for rank in (1, 2, 3):
        mate_copy(rank, other_half).wait_recv()

    sub = iota((8, PIXELS), 0).astype(jnp.float32)
    origins = [(yh + side - 2 * yh * side, lax.rem(x + NX - o, NX)) for side, o in ORIGINS]
    base = (z * 8).astype(jnp.float32)
    row_weights = [(half_of * 64 + column * 2).astype(jnp.float32) for half_of, column in origins]

    def score_chunk(g, late, queries, buffer, top):
        feats = tset[pl.ds(late * GROUP, GROUP), g].reshape(ROW_STEP * CHUNK_COLS, CH)
        scores = lax.dot_general(
            feats, queries, (((1,), (1,)), ((), ())), preferred_element_type=jnp.float32
        )
        buffer[...] = scores
        return jnp.maximum(top, jnp.max(scores.reshape(-1, 8, PIXELS), axis=0))

    def sum_chunk(g, weights, buffer, top, new_top, sums):
        s0, s1, s2 = sums
        fade = jnp.exp2(top - new_top)
        scores = buffer[...].reshape(ROW_STEP, CHUNK_COLS // 8, 8, PIXELS)
        raised = jnp.exp2(scores - new_top[None, None])
        by_row = jnp.sum(raised, axis=1)
        by_col = jnp.sum(raised, axis=0)
        total, col_part = weighted_tree([by_col[n] for n in range(CHUNK_COLS // 8)], (8, 16, 32))
        row_part = tree_sum([by_row[2 * n + 1] for n in range(GROUP)]) + total * base
        for n in range(GROUP):
            row_part = row_part + (by_row[2 * n] + by_row[2 * n + 1]) * weights[n]
        col_part = col_part + total * (sub + float(g * CHUNK_COLS))
        return s0 * fade + row_part, s1 * fade + col_part, s2 * fade + total

    state[0] = jnp.zeros((4, 8, PIXELS), jnp.float32)
    res[0] = jnp.zeros((8, PIXELS), jnp.float32)
    floor = jnp.full((8, PIXELS), NEG, jnp.float32)
    buffers = (even, odd)

    def item(step):
        first, second, last = step < 5, step < 9, step == LAST
        late = jnp.where(first, 0, jnp.where(second | last, 1, lax.rem(step + 1, 2)))
        k = jnp.where(first, step, jnp.where(second, step - 4, jnp.where(last, 0, lax.div(step + 1, 2))))
        return late, nth(k)

    def finish_block(o, late):
        top, s0, s1, s2 = tuple(state[o, m] for m in range(4))
        best = jnp.max(top, axis=0, keepdims=True)
        scale = jnp.exp2(top - best)
        t0 = jnp.sum(s0 * scale, axis=0, keepdims=True)
        t1 = jnp.sum(s1 * scale, axis=0, keepdims=True)
        t2 = jnp.sum(s2 * scale, axis=0, keepdims=True)

        marks = qset[o, PIXELS:].astype(jnp.float32)
        dest = jnp.concatenate(
            [marks[0:1] * 256.0 + marks[1:2], marks[2:3] * 256.0 + marks[3:4]], axis=1
        ).astype(jnp.int32)
        block, off = dest >> 10, dest & 1023
        here = ((block >> 2) & 7) == z
        at = jnp.zeros_like(block)
        for rank, (half_of, column) in enumerate(origins):
            at = jnp.where((block >> 5 == half_of) & ((block & 3) == column), rank * 16, at)
        at = jnp.where(here, at + (off >> 7) * 2, -1000) - late * (GROUP * 16)
        lanes = jnp.where(iota((CH, PIXELS), 0) == (off & 127), 1.0, 0.0).astype(jnp.bfloat16)
        table = bset[pl.ds(late * GROUP, GROUP)].reshape(GROUP * 16, CH)
        picked = jnp.dot(table, lanes, preferred_element_type=jnp.float32)
        line = iota((GROUP * 16, PIXELS), 0)
        back0 = jnp.sum(jnp.where(line == at, picked, 0.0), axis=0, keepdims=True)
        back1 = jnp.sum(jnp.where(line == at + 1, picked, 0.0), axis=0, keepdims=True)
        known = jnp.where(late == 1, res[o, 4:6], 0.0)
        back0, back1 = back0 + known[0:1], back1 + known[1:2]
        pad = jnp.zeros((2, PIXELS), jnp.float32)
        res[o] = jnp.concatenate([best, t0, t1, t2, back0, back1, pad], axis=0)

    def match_step(step, carry):
        late, o = item(step)
        before_late, before_o = item(jnp.where(step == LAST, 0, jnp.maximum(step - 1, 0)))
        alone = (step == 0) | (step == 4) | (step == LAST)
        next_late, next_o = item(jnp.where(alone, step, step + 1))

        @pl.when(step == 1)
        def _():
            query_copy(o).wait_recv()

        @pl.when((next_late == 0) & jnp.logical_not(alone))
        def _():
            query_copy(next_o).wait_recv()

        @pl.when(step == 2)
        def _():
            query_copy(3).start()

        @pl.when(step == 3)
        def _():
            query_copy(5).start()
            query_copy(4).start()

        @pl.when(step == 4)
        def _():
            for hop in (3, 4, 5, 6):
                take(hop)

        @pl.when(step == 5)
        def _():
            for rank in range(GROUP, BLOCKS):
                mate_copy(rank, other_half).wait_recv()

        queries, next_queries = qset[o, :PIXELS], qset[next_o, :PIXELS]

        @pl.when((step == 0) | (step == 1) | (step == 5))
        def _():
            first_top[...] = score_chunk(0, late, queries, even, floor)

        @pl.when(step == LAST)
        def _():
            done_late, done_o = item(LAST - 1)
            finish_block(done_o, done_late)
            result_copy(done_o).start()

        next_top = first_top[...]
        finish_block(before_o, before_late)
        weights = [jnp.where(late == 1, b, a) for a, b in zip(row_weights[:GROUP], row_weights[GROUP:])]
        top = jnp.where(late == 1, state[o, 0], floor)
        sums = tuple(jnp.where(late == 1, state[o, m], 0.0) for m in range(1, 4))
        next_top = jnp.maximum(next_top, top)
        for g in range(CHUNKS):
            last, top = top, next_top
            if g + 1 < CHUNKS:
                next_top = score_chunk(g + 1, late, queries, buffers[(g + 1) % 2], top)
            else:
                next_top = score_chunk(0, next_late, next_queries, even, floor)
            sums = sum_chunk(g, weights, buffers[g % 2], last, top, sums)
        state[o, 0] = top
        for m in range(3):
            state[o, m + 1] = sums[m]

        first_top[...] = next_top

        @pl.when((step > 0) & (before_late == 1) & (before_o > 0))
        def _():
            result_copy(before_o).start()

        return carry

    lax.fori_loop(0, 2 * BLOCKS, match_step, 0)
    finish_block(0, 1)

    for n in range(NZ - 1):
        block_copy(n).wait_send()
        back_copy(n).wait_send()
        mate_copy(n + 1, half).wait_send()

    def finish(o, carry):
        query_copy(o).wait_send()
        result_copy(o).wait_send()
        return carry

    lax.fori_loop(1, BLOCKS, finish, 0)

    def settle(n, carry):
        remote(res.at[n], rset.at[n], r_send.at[n], r_recv.at[n], mate).wait_recv()
        return carry

    lax.fori_loop(1, BLOCKS, settle, 0)
    parts = [res[0]] + [rset[n] for n in range(1, BLOCKS)]
    best = parts[0]
    for part in parts[1:]:
        best = jnp.maximum(best, part)
    best = best[0:1]
    total = jnp.zeros((8, PIXELS), jnp.float32)
    back = jnp.zeros((8, PIXELS), jnp.float32)
    for part in parts:
        total = total + part * jnp.exp2(part[0:1] - best)
        back = back + part
    p = iota((1, PIXELS), 1)
    row = (pb * TILE_ROWS + ((p >> 2) & 31)).astype(jnp.float32) / FRAME_ROWS
    col = (ta * TILE_COLS + (p >> 7) * 4 + (p & 3)).astype(jnp.float32) / FRAME_COLS
    flow0 = total[1:2] / total[3:4] / FRAME_ROWS - row
    flow1 = total[2:3] / total[3:4] / FRAME_COLS - col
    back0, back1 = back[4:5], back[5:6]
    diff = (flow0 + back0) ** 2 + (flow1 + back1) ** 2
    mag = flow0**2 + flow1**2 + back0**2 + back1**2
    cons = jnp.exp(-diff / (FLOW_ALPHA * mag + FLOW_BETA))
    moved = []
    for value in (flow0, flow1, cons):
        for _ in range(3):
            part = value.astype(jnp.bfloat16).astype(jnp.float32)
            moved.append(jnp.where(col_of, part, 0.0))
            value = value - part
    moved = lax.dot_general(
        jnp.concatenate(moved, axis=0).astype(jnp.bfloat16), row_hot, (((1,), (1,)), ((), ())),
        preferred_element_type=jnp.float32,
    )
    moved = [moved[n * TILE_COLS : (n + 1) * TILE_COLS] for n in range(9)]
    flow_ref[0] = moved[0] + moved[1] + moved[2]
    flow_ref[1] = moved[3] + moved[4] + moved[5]
    cons_ref[...] = moved[6] + moved[7] + moved[8]


def shards(source_feats, target_feats, back_flow, attn_weights, norm_gain, fetch_list, dest_local):
    vmem = pl.BlockSpec(memory_space=pltpu.VMEM)

    def dma(count):
        return pltpu.SemaphoreType.DMA((count,))

    args = (
        source_feats.reshape(PIXELS, CH), target_feats, back_flow, attn_weights, norm_gain, fetch_list, dest_local.T,
    )
    flow, cons = pl.pallas_call(
        kernel,
        out_shape=(
            pltpu.VMEM((2, TILE_COLS, TILE_ROWS), jnp.float32),
            pltpu.VMEM((TILE_COLS, TILE_ROWS), jnp.float32),
        ),
        in_specs=[pl.BlockSpec(memory_space=pl.ANY)] * len(args),
        out_specs=(vmem, vmem),
        scratch_shapes=[pltpu.VMEM(a.shape, a.dtype) for a in args]
        + [dma(len(args))]
        + [
            pltpu.VMEM((NZ, CHUNKS, 2 * CHUNK_COLS, CH), jnp.bfloat16),
            pltpu.VMEM((NZ, 16, CH), jnp.bfloat16),
            pltpu.VMEM((NZ, PIXELS + 16, CH), jnp.bfloat16),
            pltpu.VMEM((2, 320, CH), jnp.bfloat16),
            pltpu.VMEM((BLOCKS, 8, PIXELS), jnp.float32),
            pltpu.VMEM((BLOCKS, 8, PIXELS), jnp.float32),
            pltpu.VMEM((BLOCKS, 4, 8, PIXELS), jnp.float32),
            pltpu.VMEM((8, PIXELS), jnp.float32),
            pltpu.VMEM((ROW_STEP * CHUNK_COLS, PIXELS), jnp.float32),
            pltpu.VMEM((ROW_STEP * CHUNK_COLS, PIXELS), jnp.float32),
        ]
        + [dma(8)] * 12,
        compiler_params=pltpu.CompilerParams(
            collective_id=0, has_side_effects=True, vmem_limit_bytes=60 << 20
        ),
    )(*args)
    return jnp.swapaxes(flow, 1, 2), cons.T


def solution(mesh):
    placed = (
        P("pb", "ta", None),
        P(None, "ta"),
        P(None, "ta"),
        P(),
        P(),
        P(("pb", "ta"), None),
        P("pb", "ta"),
    )
    return jax.shard_map(
        shards,
        mesh=mesh,
        in_specs=placed,
        out_specs=(P(None, "pb", "ta"), P("pb", "ta")),
        check_vma=False,
    )
```

```python
import math

import jax
import jax.numpy as jnp
from jax import lax
from jax.experimental import pallas as pl
from jax.experimental.pallas import tpu as pltpu
from jax.sharding import PartitionSpec as P

MESH = pl.DeviceIdType.MESH
NORM_EPSILON = 1e-05
MATCH_GAIN = 2.0
FLOW_ALPHA = 0.01
FLOW_BETA = 0.5
CH = 128
PB, TA = 4, 64
NX, NZ = 4, 8
FRAME_ROWS, FRAME_COLS = 128, 512
TILE_ROWS, TILE_COLS = 32, 8
PIXELS = TILE_ROWS * TILE_COLS
BLOCKS = NZ
LAST = 2 * BLOCKS - 1
GROUP = 4
ROW_STEP = 2 * GROUP
ORIGINS = ((0, 0), (0, 1), (0, 3), (1, 0), (0, 2), (1, 1), (1, 3), (1, 2))
HOPS = ((0, 1, 0, 1), (0, 2, 0, -1), (0, 3, 1, 0), (2, 4, 0, -1), (1, 5, 1, 0), (2, 6, 1, 0), (3, 7, 0, 2))
CHUNKS, CHUNK_COLS = 8, 64
NEG = -1e30
SCORE_LOG2 = MATCH_GAIN / math.sqrt(CH) * math.log2(math.e)


def tree_sum(xs):
    xs = list(xs)
    while len(xs) > 1:
        xs = [xs[i] + xs[i + 1] for i in range(0, len(xs), 2)]
    return xs[0]


def weighted_tree(xs, weights):
    odd, cur = [], list(xs)
    while len(cur) > 1:
        odd.append(tree_sum(cur[1::2]))
        cur = [cur[i] + cur[i + 1] for i in range(0, len(cur), 2)]
    total = None
    for value, weight in zip(odd, weights):
        term = value * float(weight)
        total = term if total is None else total + term
    return cur[0], total


def normed(message, gain):
    center = message - jnp.mean(message, axis=-1, keepdims=True)
    spread = jnp.mean(center * center, axis=-1, keepdims=True)
    return center * lax.rsqrt(spread + NORM_EPSILON) * gain


def attend(queries, keys, values, admitted):
    scores = lax.dot_general(
        queries, keys, (((1,), (1,)), ((), ())), preferred_element_type=jnp.float32
    ) * (1.0 / math.sqrt(CH))
    scores = jnp.where(admitted, scores, NEG)
    raised = jnp.exp(scores - jnp.max(scores, axis=-1, keepdims=True))
    weights = (raised / jnp.sum(raised, axis=-1, keepdims=True)).astype(jnp.bfloat16)
    return jnp.dot(weights, values, preferred_element_type=jnp.float32).astype(jnp.bfloat16)


def project(pixels, matrix):
    return jnp.dot(pixels, matrix, preferred_element_type=jnp.float32).astype(jnp.bfloat16)


def iota(shape, axis):
    return lax.broadcasted_iota(jnp.int32, shape, axis)


def place():
    pb, ta = lax.axis_index("pb"), lax.axis_index("ta")
    yh, z, x = lax.div(ta, 32), lax.rem(lax.div(ta, NX), NZ), lax.rem(ta, NX)
    return pb, ta, yh, z, x


def kernel(
    src_hbm, tgt_hbm, back_hbm, w_hbm, gain_hbm, fetch_hbm, dest_hbm, flow_ref, cons_ref,
    src_ref, tgt_ref, back_ref, w_ref, gain_ref, fetch_ref, dest_ref, load_sem,
    tset, bset, qset, halo, res, rset, state, first_top, even, odd,
    t_send, t_recv, f_send, f_recv, b_send, b_recv,
    q_send, q_recv, r_send, r_recv, h_send, h_recv,
):
    pb, ta, yh, z, x = place()
    core = lax.rem(pb, 2)
    mate = (pb + 1 - 2 * core, ta)
    up, down = lax.rem(pb + PB - 1, PB), lax.rem(pb + 1, PB)
    left, right = lax.rem(ta + TA - 1, TA), lax.rem(ta + 1, TA)

    def z_peer(offset):
        return (pb, yh * 32 + lax.rem(z + offset + NZ, NZ) * NX + x)

    def x_peer(side, offset):
        far = core + 2 * (1 - lax.div(pb, 2))
        half = yh + side - 2 * yh * side
        return (pb + side * (far - pb), half * 32 + z * NX + lax.rem(x + offset + NX, NX))

    def remote(src, dst, send, recv, device):
        return pltpu.make_async_remote_copy(
            src_ref=src, dst_ref=dst, send_sem=send, recv_sem=recv, device_id=device, device_id_type=MESH
        )

    halo_copies = [
        remote(halo.at[:, 16:32], halo.at[:, 144:160], h_send.at[0], h_recv.at[0], (up, ta)),
        remote(halo.at[:, 128:144], halo.at[:, 0:16], h_send.at[1], h_recv.at[1], (down, ta)),
        remote(halo.at[1, 16:144], halo.at[0, 176:304], h_send.at[2], h_recv.at[2], (pb, right)),
        remote(halo.at[0, 16:144], halo.at[1, 176:304], h_send.at[3], h_recv.at[3], (pb, left)),
        remote(halo.at[1, 16:32], halo.at[0, 304:320], h_send.at[4], h_recv.at[4], (up, right)),
        remote(halo.at[1, 128:144], halo.at[0, 160:176], h_send.at[5], h_recv.at[5], (down, right)),
        remote(halo.at[0, 16:32], halo.at[1, 304:320], h_send.at[6], h_recv.at[6], (up, left)),
        remote(halo.at[0, 128:144], halo.at[1, 160:176], h_send.at[7], h_recv.at[7], (down, left)),
    ]

    loads = [
        pltpu.make_async_copy(a, b, load_sem.at[n])
        for n, (a, b) in enumerate(
            (
                (tgt_hbm, tgt_ref), (back_hbm, back_ref), (src_hbm, src_ref), (w_hbm, w_ref),
                (gain_hbm, gain_ref), (fetch_hbm, fetch_ref), (dest_hbm, dest_ref),
            )
        )
    ]

    barrier = pltpu.get_barrier_semaphore()
    for device in (
        (up, ta), (down, ta), (pb, right), (pb, left), (up, right), (down, right), (up, left), (down, left), mate,
        x_peer(0, 1), x_peer(0, 2), x_peer(0, 3), x_peer(1, 0),
    ):
        pl.semaphore_signal(barrier, inc=1, device_id=device, device_id_type=MESH)

    def greet(o, carry):
        pl.semaphore_signal(barrier, inc=1, device_id=z_peer(o), device_id_type=MESH)
        return carry

    lax.fori_loop(1, NZ, greet, 0)

    for copy in loads:
        copy.start()

    half = pl.ds(core * (CHUNKS // 2), CHUNKS // 2)
    other_half = pl.ds((1 - core) * (CHUNKS // 2), CHUNKS // 2)

    def block_copy(n):
        held, rank, side, steps = HOPS[n]
        return remote(tset.at[held, half], tset.at[rank, half], t_send.at[n], t_recv.at[rank], x_peer(side, steps))

    def back_copy(n):
        held, rank, side, steps = HOPS[n]
        return remote(bset.at[held], bset.at[rank], b_send.at[n], b_recv.at[rank], x_peer(side, steps))

    def mate_copy(rank, part):
        return remote(tset.at[rank, part], tset.at[rank, part], f_send.at[rank], f_recv.at[rank], mate)

    def pass_on(n):
        block_copy(n).start()
        back_copy(n).start()

    def take(n):
        block_copy(n).wait_recv()
        back_copy(n).wait_recv()
        mate_copy(HOPS[n][1], half).start()

    for copy in loads[:2]:
        copy.wait()
    turned = tgt_ref[...].T
    for g in range(CHUNKS):
        for r in range(2):
            at = r * FRAME_COLS + g * CHUNK_COLS
            tset[0, g, r * CHUNK_COLS : (r + 1) * CHUNK_COLS] = turned[at : at + CHUNK_COLS]
    back = back_ref[...].astype(jnp.float32)
    bset[0] = jnp.concatenate([back[:, CH * n : CH * n + CH] for n in range(8)], axis=0).astype(jnp.bfloat16)
    for copy in loads[2:]:
        copy.wait()
    picks = dest_ref[...]
    listed = jnp.zeros_like(picks)
    for n in range(4):
        listed = jnp.where((picks >> 10) == n, fetch_ref[0:1, n : n + 1], listed)
    dests = listed * 1024 + (picks & 1023)
    pixel = iota((TILE_ROWS, PIXELS), 1)
    row_of = ((pixel >> 2) & 31) == iota((TILE_ROWS, PIXELS), 0)
    row_hot = jnp.where(row_of, 1.0, 0.0).astype(jnp.bfloat16)
    pixel = iota((TILE_COLS, PIXELS), 1)
    col_of = (pixel >> 7) * 4 + (pixel & 3) == iota((TILE_COLS, PIXELS), 0)
    spread = [
        jnp.dot(part.astype(jnp.float32).astype(jnp.bfloat16), row_hot, preferred_element_type=jnp.float32)
        for part in (dests >> 8, dests & 255)
    ]
    spread = jnp.where(col_of, spread[0] * 256.0 + spread[1], 0.0)
    spread = jnp.sum(spread, axis=0, keepdims=True)
    coarse = jnp.floor(spread * (1.0 / 256.0))
    pair = jnp.concatenate([coarse, spread - coarse * 256.0], axis=0)
    qset[0, PIXELS:] = jnp.concatenate(
        [pair[:, :CH], pair[:, CH:], jnp.zeros((12, CH), jnp.float32)], axis=0
    ).astype(jnp.bfloat16)

    i = iota((PIXELS, PIXELS), 0)
    j = iota((PIXELS, PIXELS), 1)
    wanted = ((i >> 2) & 31) * 8 + (i >> 7) * 4 + (i & 3)
    order = jnp.where(wanted == j, 1.0, 0.0).astype(jnp.bfloat16)
    pixels = project(order, src_ref[...])
    same = ((i >> 5) & 3) == ((j >> 5) & 3)
    attended = attend(
        project(pixels, w_ref[0, 0]), project(pixels, w_ref[0, 1]), project(pixels, w_ref[0, 2]), same
    )
    message = jnp.dot(attended, w_ref[0, 3], preferred_element_type=jnp.float32)
    one = (pixels.astype(jnp.float32) + normed(message, gain_ref[0:1])).astype(jnp.bfloat16)
    halo[0, 16:144] = one[:128]
    halo[1, 16:144] = one[128:]
    pl.semaphore_wait(barrier, 13 + (BLOCKS - 1))
    for copy in halo_copies:
        copy.start()
    for n in (0, 1, 2):
        pass_on(n)

    i = iota((128, 320), 0)
    j = iota((128, 320), 1)
    beside = j >= 160
    kk = jnp.where(beside, j - 160, j)
    row, key_row = i >> 2, (kk >> 2) - 4
    low = pb * TILE_ROWS + row < 4
    key_low = ((pb * TILE_ROWS + key_row + FRAME_ROWS) & (FRAME_ROWS - 1)) < 4
    rows_agree = (((row + 4) >> 3) == (kk >> 5)) & (low == key_low)
    admitted = [rows_agree & jnp.logical_not(beside & (ta == edge)) for edge in (0, TA - 1)]
    own_queries = [project(one[h * 128 : (h + 1) * 128], w_ref[1, 0]) for h in range(2)]
    for copy in halo_copies:
        copy.wait()
    for h in range(2):
        around = halo[h]
        own = halo[h, 16:144]
        attended = attend(
            own_queries[h], project(around, w_ref[1, 1]), project(around, w_ref[1, 2]), admitted[h]
        )
        message = jnp.dot(attended, w_ref[1, 3], preferred_element_type=jnp.float32)
        two = (own.astype(jnp.float32) + normed(message, gain_ref[1:2])).astype(jnp.bfloat16)
        qset[0, h * 128 : (h + 1) * 128] = (two.astype(jnp.float32) * SCORE_LOG2).astype(jnp.bfloat16)

    def nth(k):
        odd = lax.rem(k, 2)
        return lax.rem(odd * lax.div(k + 1, 2) + (1 - odd) * (NZ - lax.div(k, 2)), NZ)

    def query_copy(o):
        held = jnp.where((o == 3) | (o == 4), 2, jnp.where(o == 5, 6, 0))
        return remote(qset.at[held], qset.at[o], q_send.at[o], q_recv.at[o], z_peer(lax.rem(o - held + NZ, NZ)))

    def result_copy(o):
        return remote(res.at[o], rset.at[o], r_send.at[o], r_recv.at[o], z_peer(-o))

    query_copy(1).start()
    query_copy(7).start()
    query_copy(2).start()
    query_copy(6).start()
    take(0)
    pass_on(4)
    take(1)
    pass_on(3)
    pass_on(5)
    take(2)
    pass_on(6)
    for rank in (1, 2, 3):
        mate_copy(rank, other_half).wait_recv()

    sub = iota((8, PIXELS), 0).astype(jnp.float32)
    origins = [(yh + side - 2 * yh * side, lax.rem(x + NX - o, NX)) for side, o in ORIGINS]
    base = (z * 8).astype(jnp.float32)
    row_weights = [(half_of * 64 + column * 2).astype(jnp.float32) for half_of, column in origins]

    def score_chunk(g, late, queries, buffer, top):
        feats = tset[pl.ds(late * GROUP, GROUP), g].reshape(ROW_STEP * CHUNK_COLS, CH)
        scores = lax.dot_general(
            feats, queries, (((1,), (1,)), ((), ())), preferred_element_type=jnp.float32
        )
        buffer[...] = scores
        return jnp.maximum(top, jnp.max(scores.reshape(-1, 8, PIXELS), axis=0))

    def sum_chunk(g, weights, buffer, top, new_top, sums):
        s0, s1, s2 = sums
        fade = jnp.exp2(top - new_top)
        scores = buffer[...].reshape(ROW_STEP, CHUNK_COLS // 8, 8, PIXELS)
        raised = jnp.exp2(scores - new_top[None, None])
        by_row = jnp.sum(raised, axis=1)
        by_col = jnp.sum(raised, axis=0)
        total, col_part = weighted_tree([by_col[n] for n in range(CHUNK_COLS // 8)], (8, 16, 32))
        row_part = tree_sum([by_row[2 * n + 1] for n in range(GROUP)]) + total * base
        for n in range(GROUP):
            row_part = row_part + (by_row[2 * n] + by_row[2 * n + 1]) * weights[n]
        col_part = col_part + total * (sub + float(g * CHUNK_COLS))
        return s0 * fade + row_part, s1 * fade + col_part, s2 * fade + total

    state[0] = jnp.zeros((4, 8, PIXELS), jnp.float32)
    res[0] = jnp.zeros((8, PIXELS), jnp.float32)
    floor = jnp.full((8, PIXELS), NEG, jnp.float32)
    buffers = (even, odd)

    def item(step):
        first, second, last = step < 5, step < 9, step == LAST
        late = jnp.where(first, 0, jnp.where(second | last, 1, lax.rem(step + 1, 2)))
        k = jnp.where(first, step, jnp.where(second, step - 4, jnp.where(last, 0, lax.div(step + 1, 2))))
        return late, nth(k)

    def finish_block(o, late):
        top, s0, s1, s2 = tuple(state[o, m] for m in range(4))
        best = jnp.max(top, axis=0, keepdims=True)
        scale = jnp.exp2(top - best)
        t0 = jnp.sum(s0 * scale, axis=0, keepdims=True)
        t1 = jnp.sum(s1 * scale, axis=0, keepdims=True)
        t2 = jnp.sum(s2 * scale, axis=0, keepdims=True)

        marks = qset[o, PIXELS:].astype(jnp.float32)
        dest = jnp.concatenate(
            [marks[0:1] * 256.0 + marks[1:2], marks[2:3] * 256.0 + marks[3:4]], axis=1
        ).astype(jnp.int32)
        block, off = dest >> 10, dest & 1023
        here = ((block >> 2) & 7) == z
        at = jnp.zeros_like(block)
        for rank, (half_of, column) in enumerate(origins):
            at = jnp.where((block >> 5 == half_of) & ((block & 3) == column), rank * 16, at)
        at = jnp.where(here, at + (off >> 7) * 2, -1000) - late * (GROUP * 16)
        lanes = jnp.where(iota((CH, PIXELS), 0) == (off & 127), 1.0, 0.0).astype(jnp.bfloat16)
        table = bset[pl.ds(late * GROUP, GROUP)].reshape(GROUP * 16, CH)
        picked = jnp.dot(table, lanes, preferred_element_type=jnp.float32)
        line = iota((GROUP * 16, PIXELS), 0)
        back0 = jnp.sum(jnp.where(line == at, picked, 0.0), axis=0, keepdims=True)
        back1 = jnp.sum(jnp.where(line == at + 1, picked, 0.0), axis=0, keepdims=True)
        known = jnp.where(late == 1, res[o, 4:6], 0.0)
        back0, back1 = back0 + known[0:1], back1 + known[1:2]
        pad = jnp.zeros((2, PIXELS), jnp.float32)
        res[o] = jnp.concatenate([best, t0, t1, t2, back0, back1, pad], axis=0)

    def match_step(step, carry):
        late, o = item(step)
        before_late, before_o = item(jnp.where(step == LAST, 0, jnp.maximum(step - 1, 0)))
        alone = (step == 0) | (step == 4) | (step == LAST)
        next_late, next_o = item(jnp.where(alone, step, step + 1))

        @pl.when(step == 1)
        def _():
            query_copy(o).wait_recv()

        @pl.when((next_late == 0) & jnp.logical_not(alone))
        def _():
            query_copy(next_o).wait_recv()

        @pl.when(step == 2)
        def _():
            query_copy(3).start()
            query_copy(4).start()

        @pl.when(step == 3)
        def _():
            query_copy(5).start()

        @pl.when(step == 4)
        def _():
            for hop in (3, 4, 5, 6):
                take(hop)

        @pl.when(step == 5)
        def _():
            for rank in range(GROUP, BLOCKS):
                mate_copy(rank, other_half).wait_recv()

        queries, next_queries = qset[o, :PIXELS], qset[next_o, :PIXELS]

        @pl.when((step == 0) | (step == 1) | (step == 5))
        def _():
            first_top[...] = score_chunk(0, late, queries, even, floor)

        @pl.when(step == LAST)
        def _():
            done_late, done_o = item(LAST - 1)
            finish_block(done_o, done_late)
            result_copy(done_o).start()

        next_top = first_top[...]
        finish_block(before_o, before_late)
        weights = [jnp.where(late == 1, b, a) for a, b in zip(row_weights[:GROUP], row_weights[GROUP:])]
        top = jnp.where(late == 1, state[o, 0], floor)
        sums = tuple(jnp.where(late == 1, state[o, m], 0.0) for m in range(1, 4))
        next_top = jnp.maximum(next_top, top)
        for g in range(CHUNKS):
            last, top = top, next_top
            if g + 1 < CHUNKS:
                next_top = score_chunk(g + 1, late, queries, buffers[(g + 1) % 2], top)
            else:
                next_top = score_chunk(0, next_late, next_queries, even, floor)
            sums = sum_chunk(g, weights, buffers[g % 2], last, top, sums)
        state[o, 0] = top
        for m in range(3):
            state[o, m + 1] = sums[m]

        first_top[...] = next_top

        @pl.when((step > 0) & (before_late == 1) & (before_o > 0))
        def _():
            result_copy(before_o).start()

        return carry

    lax.fori_loop(0, 2 * BLOCKS, match_step, 0)
    finish_block(0, 1)

    for n in range(NZ - 1):
        block_copy(n).wait_send()
        back_copy(n).wait_send()
        mate_copy(n + 1, half).wait_send()

    def finish(o, carry):
        query_copy(o).wait_send()
        result_copy(o).wait_send()
        return carry

    lax.fori_loop(1, BLOCKS, finish, 0)

    def settle(n, carry):
        remote(res.at[n], rset.at[n], r_send.at[n], r_recv.at[n], mate).wait_recv()
        return carry

    lax.fori_loop(1, BLOCKS, settle, 0)
    parts = [res[0]] + [rset[n] for n in range(1, BLOCKS)]
    best = parts[0]
    for part in parts[1:]:
        best = jnp.maximum(best, part)
    best = best[0:1]
    total = jnp.zeros((8, PIXELS), jnp.float32)
    back = jnp.zeros((8, PIXELS), jnp.float32)
    for part in parts:
        total = total + part * jnp.exp2(part[0:1] - best)
        back = back + part
    p = iota((1, PIXELS), 1)
    row = (pb * TILE_ROWS + ((p >> 2) & 31)).astype(jnp.float32) / FRAME_ROWS
    col = (ta * TILE_COLS + (p >> 7) * 4 + (p & 3)).astype(jnp.float32) / FRAME_COLS
    flow0 = total[1:2] / total[3:4] / FRAME_ROWS - row
    flow1 = total[2:3] / total[3:4] / FRAME_COLS - col
    back0, back1 = back[4:5], back[5:6]
    diff = (flow0 + back0) ** 2 + (flow1 + back1) ** 2
    mag = flow0**2 + flow1**2 + back0**2 + back1**2
    cons = jnp.exp(-diff / (FLOW_ALPHA * mag + FLOW_BETA))
    moved = []
    for value in (flow0, flow1, cons):
        for _ in range(3):
            part = value.astype(jnp.bfloat16).astype(jnp.float32)
            moved.append(jnp.where(col_of, part, 0.0))
            value = value - part
    moved = lax.dot_general(
        jnp.concatenate(moved, axis=0).astype(jnp.bfloat16), row_hot, (((1,), (1,)), ((), ())),
        preferred_element_type=jnp.float32,
    )
    moved = [moved[n * TILE_COLS : (n + 1) * TILE_COLS] for n in range(9)]
    flow_ref[0] = moved[0] + moved[1] + moved[2]
    flow_ref[1] = moved[3] + moved[4] + moved[5]
    cons_ref[...] = moved[6] + moved[7] + moved[8]


def shards(source_feats, target_feats, back_flow, attn_weights, norm_gain, fetch_list, dest_local):
    vmem = pl.BlockSpec(memory_space=pltpu.VMEM)

    def dma(count):
        return pltpu.SemaphoreType.DMA((count,))

    args = (
        source_feats.reshape(PIXELS, CH), target_feats, back_flow, attn_weights, norm_gain, fetch_list, dest_local.T,
    )
    flow, cons = pl.pallas_call(
        kernel,
        out_shape=(
            pltpu.VMEM((2, TILE_COLS, TILE_ROWS), jnp.float32),
            pltpu.VMEM((TILE_COLS, TILE_ROWS), jnp.float32),
        ),
        in_specs=[pl.BlockSpec(memory_space=pl.ANY)] * len(args),
        out_specs=(vmem, vmem),
        scratch_shapes=[pltpu.VMEM(a.shape, a.dtype) for a in args]
        + [dma(len(args))]
        + [
            pltpu.VMEM((NZ, CHUNKS, 2 * CHUNK_COLS, CH), jnp.bfloat16),
            pltpu.VMEM((NZ, 16, CH), jnp.bfloat16),
            pltpu.VMEM((NZ, PIXELS + 16, CH), jnp.bfloat16),
            pltpu.VMEM((2, 320, CH), jnp.bfloat16),
            pltpu.VMEM((BLOCKS, 8, PIXELS), jnp.float32),
            pltpu.VMEM((BLOCKS, 8, PIXELS), jnp.float32),
            pltpu.VMEM((BLOCKS, 4, 8, PIXELS), jnp.float32),
            pltpu.VMEM((8, PIXELS), jnp.float32),
            pltpu.VMEM((ROW_STEP * CHUNK_COLS, PIXELS), jnp.float32),
            pltpu.VMEM((ROW_STEP * CHUNK_COLS, PIXELS), jnp.float32),
        ]
        + [dma(8)] * 12,
        compiler_params=pltpu.CompilerParams(
            collective_id=0, has_side_effects=True, vmem_limit_bytes=60 << 20
        ),
    )(*args)
    return jnp.swapaxes(flow, 1, 2), cons.T


def solution(mesh):
    placed = (
        P("pb", "ta", None),
        P(None, "ta"),
        P(None, "ta"),
        P(),
        P(),
        P(("pb", "ta"), None),
        P("pb", "ta"),
    )
    return jax.shard_map(
        shards,
        mesh=mesh,
        in_specs=placed,
        out_specs=(P(None, "pb", "ta"), P("pb", "ta")),
        check_vma=False,
    )
```
